128 devices in a mesh: gx: 2 (over core), gy: 16 (over y, x), gz: 4 (over z).
Axes of the slice: x: 4, y: 4, z: 4, core: 2. Of those that a mesh axis runs over, the one named last changes fastest.
Arguments:
- species_field: float32 [48, 2048, 2048], P('gz', 'gx', 'gy')
- x_mode_basis: float32 [2048, 256], P('gx'), may hold values from -0.125 to 0.125
- y_mode_basis: float32 [2048, 256], P('gy'), may hold values from -0.125 to 0.125
Outputs:
- gram_x: float32 [2048, 2048], P(('gx', 'gy'))
- gram_y: float32 [2048, 2048], P('gy', 'gx')
- reduced_core_tensor: float32 [256, 48, 256], P('gx', 'gz', 'gy')
The draws below stay inside these ranges and needn't reach their ends.
All inputs are finite; a program needn't handle non-finite values.
Results may differ from the reference program's by a relative error of at most 0.000092.
Values sent between devices are 32-bit elements; how exact they have to be, the bound alone decides.
No kernel may reach another device: no remote copies, remote signals or barrier semaphores. Data moves between devices by JAX's collectives and lax.ppermute only.
A program may use at most 128 MiB of HBM per device.

```python
import math
import jax
import jax.numpy as jnp
from jax import lax

NX = 2048
NY = 2048
SPECIES = 24
PLANES = 2
R = 256
RY = 256


def draw_species_field(key, part):
    key = jax.random.fold_in(key, 11)
    keys = jax.random.split(key, 4)
    slices = SPECIES * PLANES
    spread = math.log(2.0)
    noise_part = jax.random.normal(keys[0], (slices, NX, NY), jnp.float32)
    row_scale_factors = jnp.exp(jax.random.uniform(keys[1], (1, NX, 1), jnp.float32, -spread, spread))
    scale_cols = jnp.exp(jax.random.uniform(keys[2], (1, 1, NY), jnp.float32, -spread, spread))
    scale_slices = jnp.exp(jax.random.uniform(keys[3], (slices, 1, 1), jnp.float32, -spread, spread))
    return noise_part * row_scale_factors * scale_cols * scale_slices


def level_of(stream_key, shape, pieces, smallest, largest):
    level, own = 1.0, jax.random.fold_in(stream_key, 6)
    for dim, parts in pieces:
        steps = jnp.exp(jax.random.uniform(jax.random.fold_in(own, dim), (parts,), jnp.float32, smallest / len(pieces), largest / len(pieces)))
        level = level * jnp.repeat(steps, shape[dim] // parts).reshape([-1 if axis == dim else 1 for axis in range(len(shape))])
    return level


def noise(stream_key, dims, deviation, limit, pieces=(), kind=jnp.bfloat16):
    values = deviation * jax.random.normal(stream_key, dims, jnp.float32)
    if pieces:
        values = values * level_of(stream_key, dims, pieces, -0.22, 0.18)
    return jnp.clip(values, -limit, limit).astype(kind)


def setup_inputs(seed: int = 0) -> dict:
    splits = jax.random.split(jax.random.key(seed), 4)
    return {
        "species_field": draw_species_field(jax.random.fold_in(splits[3], 71), 0),
        "x_mode_basis": noise(splits[1], (NX, R), NX ** -0.5, 0.125, ((0, 2),), jnp.float32),
        "y_mode_basis": noise(splits[2], (NY, RY), NY ** -0.5, 0.125, ((0, 16),), jnp.float32),
    }


def reference(species_field, x_mode_basis, y_mode_basis):
    exact_precision = lax.Precision.HIGHEST
    slices = SPECIES * PLANES
    gram_x = jnp.einsum("sxy,szy->xz", species_field, species_field, precision=exact_precision) / (NY * slices)
    reduced_result = jnp.einsum("xr,sxy->rsy", x_mode_basis, species_field, precision=exact_precision)
    gram_y = jnp.einsum("rsy,rsz->yz", reduced_result, reduced_result, precision=exact_precision) / (R * slices)
    reduced_core_tensor = jnp.einsum("mtl,lw->mtw", reduced_result, y_mode_basis, precision=exact_precision)
    return (gram_x, gram_y, reduced_core_tensor)
```

```python
import functools

import jax
import jax.numpy as jnp
from jax import lax
from jax.experimental import pallas as pl
from jax.experimental.pallas import tpu as pltpu
from jax.sharding import PartitionSpec as P

F32 = jnp.float32
BF16 = jnp.bfloat16
VMEM_LIMIT = 58 * 1024 * 1024

PERM_X = {d: [(y * 4 + x, y * 4 + (x + d) % 4) for y in range(4) for x in range(4)] for d in (1, 2, 3)}
PERM_Y = {d: [(y * 4 + x, (y + d) % 4 * 4 + x) for y in range(4) for x in range(4)] for d in (1, 2, 3)}
PERM_Z = {d: [(z, (z + d) % 4) for z in range(4)] for d in (1, 2, 3)}
SWAP = [(0, 1), (1, 0)]


def shift_x(v, d):
    return lax.ppermute(v, "gy", PERM_X[d])


def shift_y(v, d):
    return lax.ppermute(v, "gy", PERM_Y[d])


def shift_z(v, d):
    return lax.ppermute(v, "gz", PERM_Z[d])


def split(v):
    high = v.astype(BF16)
    return high, (v - high.astype(F32)).astype(BF16)


def dot3(a_high, a_low, b_high, b_low, dims):
    dot = functools.partial(lax.dot_general, dimension_numbers=(dims, ((), ())), preferred_element_type=F32)
    return dot(a_high, b_high) + (dot(a_high, b_low) + dot(a_low, b_high))


def project_kernel(field, basis, own, other):
    f_high, f_low = split(jnp.concatenate([field[0], field[1]], axis=1))
    x_high, x_low = split(basis[...])
    out = dot3(x_high, x_low, f_high, f_low, ((1,), (0,)))
    own[...] = out[:128]
    other[...] = out[128:]


def project(field, basis_t):
    out = jax.ShapeDtypeStruct((128, 1536), F32)
    return pl.pallas_call(
        project_kernel,
        grid=(6,),
        in_specs=[
            pl.BlockSpec((2, 1024, 128), lambda i: (i, 0, 0)),
            pl.BlockSpec((256, 1024), lambda i: (0, 0)),
        ],
        out_specs=[pl.BlockSpec((128, 256), lambda i: (0, i))] * 2,
        out_shape=[out, out],
        compiler_params=pltpu.CompilerParams(vmem_limit_bytes=VMEM_LIMIT),
        cost_estimate=pl.CostEstimate(flops=2400000000, bytes_accessed=9000000, transcendentals=0),
        name="project",
    )(field, basis_t)


def emit_pieces(place, buf, dy, lane_of, a_refs, b_refs, c_refs):
    x0, z0 = place[1], place[3]
    for dx in range(4):
        x = lax.rem(x0 + dx, 4)
        lane = pl.multiple_of(lane_of(x), 128)
        for dz in range(4):
            z = lax.rem(z0 + dz, 4)
            row = pl.multiple_of(x * 64 + z * 16, 16)
            a_refs[dx][dy, dz] = buf[pl.ds(row, 16), pl.ds(lane, 384)]
            b_refs[dy][dz, dx] = buf[pl.ds(row, 16), pl.ds(lane + 384, 384)]
            c_refs[dz][dx, dy] = buf[pl.ds(row, 16), pl.ds(lane + 768, 384)]


def gram_x_kernel(place, own, other, *refs):
    a_refs, b_refs, c_refs = refs[0:4], refs[4:8], refs[8:12]
    high, low, buf = refs[12:]
    for half, src in enumerate((own, other)):
        for s in range(12):
            v_high, v_low = split(src[s])
            high[half * 1024 : half * 1024 + 1024, s * 128 : s * 128 + 128] = v_high
            low[half * 1024 : half * 1024 + 1024, s * 128 : s * 128 + 128] = v_low
    y0 = place[2]
    for dy in range(4):
        b = lax.rem(y0 + dy, 4)
        rows = pl.ds(pl.multiple_of(b * 256, 256), 256)

        @pl.loop(0, 5)
        def _(n):
            cols = pl.ds(pl.multiple_of((b + n) * 256, 256), 256)
            buf[:, pl.ds(pl.multiple_of(n * 256, 256), 256)] = dot3(
                high[rows, :], low[rows, :], high[cols, :], low[cols, :], ((1,), (1,))
            )

        emit_pieces(place, buf, dy, lambda x: (x // 2) * 128, a_refs, b_refs, c_refs)


def gram_y_kernel(place, own, other, *refs):
    a_refs, b_refs, c_refs = refs[0:4], refs[4:8], refs[8:12]
    high, low, buf = refs[12:]
    for j in range(16):
        tiles = [src[j, :, s * 128 : s * 128 + 128] for src in (own, other) for s in range(12)]
        v = jnp.concatenate(tiles + [jnp.zeros((64, 128), F32)], axis=0).T
        v_high, v_low = split(v)
        for start in (j * 128, 2048 + j * 128):
            if start < 3072:
                high[start : start + 128, :] = v_high
                low[start : start + 128, :] = v_low
    h, y0 = place[0], place[2]
    for dy in range(4):
        b = lax.rem(y0 + dy, 4)
        starts = [pl.multiple_of((b * 4 + x) * 128 + h * 64, 64) for x in range(4)]
        l_high = jnp.concatenate([high[pl.ds(r, 64), :] for r in starts], axis=0)
        l_low = jnp.concatenate([low[pl.ds(r, 64), :] for r in starts], axis=0)
        for n in range(6):
            cols = pl.ds(pl.multiple_of(b * 512 + n * 256, 256), 256)
            buf[:, n * 256 : n * 256 + 256] = dot3(l_high, l_low, high[cols, :], low[cols, :], ((1,), (1,)))
        emit_pieces(place, buf, dy, lambda x: x * 128, a_refs, b_refs, c_refs)


def gram_pieces(kernel, name, place, own, other, scratch, flops):
    out = jax.ShapeDtypeStruct((4, 4, 16, 384), F32)
    whole = pl.BlockSpec(memory_space=pltpu.VMEM)
    outs = pl.pallas_call(
        kernel,
        in_specs=[pl.BlockSpec(memory_space=pltpu.SMEM), whole, whole],
        out_specs=[whole] * 12,
        out_shape=[out] * 12,
        scratch_shapes=scratch,
        compiler_params=pltpu.CompilerParams(vmem_limit_bytes=VMEM_LIMIT),
        cost_estimate=pl.CostEstimate(flops=flops, bytes_accessed=20000000, transcendentals=0),
        name=name,
    )(place, own, other)
    return outs[0:4], outs[4:8], outs[8:12]


def exchange(pieces, shift):
    return [pieces[0]] + [shift(pieces[d], d) for d in (1, 2, 3)]


def total(terms):
    return (terms[0] + terms[1]) + (terms[2] + terms[3])


def rolled(v, start):
    return lax.dynamic_slice_in_dim(jnp.concatenate([v, v], axis=0), start, v.shape[0], axis=0)


def per_device(species_field, x_mode_basis, y_mode_basis):
    h, j, z0 = lax.axis_index("gx"), lax.axis_index("gy"), lax.axis_index("gz")
    x0, y0 = j % 4, j // 4
    place = jnp.stack([h, x0, y0, z0]).astype(jnp.int32)
    nx = 2 * species_field.shape[1]
    ny = 16 * species_field.shape[2]
    slices = 4 * species_field.shape[0]
    ranks = x_mode_basis.shape[1]

    other_field = lax.ppermute(species_field, "gx", SWAP)
    basis_t = x_mode_basis.T
    basis_t = jnp.where(h == 0, basis_t, jnp.concatenate([basis_t[128:], basis_t[:128]], axis=0))
    mine, theirs = project(species_field, basis_t)
    reduced = mine + lax.ppermute(theirs, "gx", SWAP)
    fibers = lax.all_to_all(reduced.reshape(16, 8, 1536), "gy", 0, 0, tiled=True)
    other_fibers = lax.ppermute(fibers, "gx", SWAP)

    gx_a, gx_b, gx_c = gram_pieces(
        gram_x_kernel, "gram_x", place, species_field, other_field,
        [pltpu.VMEM((2048, 1536), BF16), pltpu.VMEM((2048, 1536), BF16), pltpu.VMEM((256, 1280), F32)], 12000000000,
    )
    gy_a, gy_b, gy_c = gram_pieces(
        gram_y_kernel, "gram_y", place, fibers, other_fibers,
        [pltpu.VMEM((3072, 256), BF16), pltpu.VMEM((3072, 256), BF16), pltpu.VMEM((256, 1536), F32)], 2400000000,
    )

    y_all = lax.all_to_all(
        jnp.broadcast_to(lax.dynamic_slice_in_dim(y_mode_basis, h * 64, 64, axis=0), (16, 64, 256)), "gy", 0, 0, tiled=True
    )
    y_other = lax.ppermute(y_all, "gx", SWAP)
    y_pair = jnp.where(h == 0, jnp.stack([y_all, y_other], axis=1), jnp.stack([y_other, y_all], axis=1))
    core = lax.dot_general(
        fibers.reshape(16, 8, 12, 128).transpose(2, 1, 0, 3).reshape(96, ny),
        y_pair.reshape(ny, 256),
        (((1,), (0,)), ((), ())),
        precision=lax.Precision.HIGH,
        preferred_element_type=F32,
    )
    core = lax.all_to_all(core.reshape(96, 16, 16).transpose(1, 0, 2).reshape(16, 12, 128), "gy", 0, 0, tiled=True)
    core = core.reshape(16, 12, 8, 16).transpose(0, 2, 1, 3).reshape(128, 12, 16)

    def first(pieces, shift):
        return exchange(pieces, shift)

    ax, bx, cx = first(gx_a, shift_x), first(gx_b, shift_y), first(gx_c, shift_z)
    ay, by, cy = first(gy_a, shift_x), first(gy_b, shift_y), first(gy_c, shift_z)

    def second(tx, ty, shift):
        parts = [jnp.stack([total([t[d] for t in tx]), total([t[d] for t in ty])], axis=1) for d in range(4)]
        return exchange(parts, shift)

    a2, b2, c2 = second(ax, ay, shift_y), second(bx, by, shift_z), second(cx, cy, shift_x)

    def third(t, shift):
        return total(exchange([total([v[d] for v in t]) for d in range(4)], shift))

    window = jnp.concatenate([third(a2, shift_z), third(b2, shift_x), third(c2, shift_y)], axis=2)

    wide = jnp.pad(window.reshape(2, 16, 9, 128).transpose(0, 2, 1, 3), ((0, 0), (0, 7), (0, 0), (0, 0)))
    block_x = h * 8 + j // 2
    direct_x = rolled(wide[0], (16 - block_x) % 16)
    direct_y = rolled(wide[1], (16 - j) % 16)
    to_x = jnp.broadcast_to(direct_x[:, None], (16, 2, 16, 128)).reshape(32, 16, 128)
    to_y = jnp.broadcast_to(direct_y[None], (2, 16, 16, 128)).reshape(32, 16, 128)
    got = lax.all_to_all(jnp.stack([to_x, to_y], axis=1), ("gx", "gy"), 0, 0, tiled=True)
    got_x = got[:, 0].reshape(16, 2, 16, 2, 64)
    got_x = jnp.where(j % 2 == 0, got_x[:, :, :, 0], got_x[:, :, :, 1]).transpose(0, 2, 1, 3).reshape(16, 16, 128)
    is_direct_x = (jnp.arange(16) - block_x) % 16 <= 8
    part_x = jnp.where(is_direct_x[:, None, None], direct_x, got_x)

    def half_of(v, k):
        return jnp.where(k == 0, v[:8], v[8:])

    keep = half_of(direct_y, h)
    come = lax.ppermute(half_of(direct_y, 1 - h), "gx", SWAP)
    direct_y = jnp.where(h == 0, jnp.stack([keep, come], axis=1), jnp.stack([come, keep], axis=1))
    got_y = jnp.stack([half_of(got[:16, 1], h), half_of(got[16:, 1], h)], axis=1)
    is_direct_y = (h * 8 + jnp.arange(8) - j) % 16 <= 8
    part_y = jnp.where(is_direct_y[:, None, None, None], direct_y, got_y)

    part = jnp.concatenate([part_x, part_y.reshape(16, 16, 128)], axis=0)
    quarters = exchange([part] * 4, shift_z)
    quarters = jnp.stack([quarters[3], quarters[2], quarters[1], quarters[0]])
    quarters = rolled(quarters, 3 - z0)

    all_x = quarters[:, :16].transpose(1, 0, 2, 3).reshape(16, 64, 128)
    turned_x = all_x.reshape(16, 64, 2, 64).transpose(0, 3, 2, 1).reshape(16, 64, 128)
    gram_x = jnp.where(is_direct_x[:, None, None], all_x, turned_x).transpose(1, 0, 2).reshape(64, nx) / (ny * slices)
    all_y = quarters[:, 16:].reshape(4, 8, 2, 16, 128).transpose(1, 2, 0, 3, 4).reshape(8, 128, 128)
    turned_y = all_y.transpose(0, 2, 1)
    gram_y = jnp.where(is_direct_y[:, None, None], all_y, turned_y).transpose(1, 0, 2).reshape(128, ny // 2) / (ranks * slices)
    return (gram_x, gram_y, core)


def solution(mesh):
    in_specs = (P("gz", "gx", "gy"), P("gx", None), P("gy", None))
    out_specs = (P(("gx", "gy"), None), P("gy", "gx"), P("gx", "gz", "gy"))
    return jax.shard_map(
        per_device, mesh=mesh, in_specs=in_specs, out_specs=out_specs, check_vma=False
    )
```

```python
import functools

import jax
import jax.numpy as jnp
from jax import lax
from jax.experimental import pallas as pl
from jax.experimental.pallas import tpu as pltpu
from jax.sharding import PartitionSpec as P

F32 = jnp.float32
BF16 = jnp.bfloat16
VMEM_LIMIT = 58 * 1024 * 1024

SWAP = [(0, 1), (1, 0)]


def device(h, y, x, z):
    return (h * 16 + y % 4 * 4 + x % 4) * 4 + z % 4


def stepper(axis):
    def step(v, d):
        pairs = []
        for h in range(2):
            by = d if h == 0 else -d
            move = [by if name == axis else 0 for name in "yxz"]
            for y in range(4):
                for x in range(4):
                    for z in range(4):
                        pairs.append((device(h, y, x, z), device(h, y + move[0], x + move[1], z + move[2])))
        return lax.ppermute(v, ("gx", "gy", "gz"), pairs)

    return step


shift_x, shift_y, shift_z = stepper("x"), stepper("y"), stepper("z")


def ahead(place, axis, d):
    return lax.rem(place[axis] + d * place[4], 4)


def split(v):
    high = v.astype(BF16)
    return high, (v - high.astype(F32)).astype(BF16)


def dot3(a_high, a_low, b_high, b_low, dims):
    dot = functools.partial(lax.dot_general, dimension_numbers=(dims, ((), ())), preferred_element_type=F32)
    return dot(a_high, b_high) + (dot(a_high, b_low) + dot(a_low, b_high))


def project_kernel(place, field, basis, own, other, land, x_land, x_high, x_low, sems):
    def load(k):
        part = pl.ds(k * 2, 2)
        return pltpu.make_async_copy(field.at[part], land.at[part], sems.at[k])

    x_load = pltpu.make_async_copy(basis, x_land, sems.at[6])
    x_load.start()
    for k in range(6):
        load(k).start()
    x_load.wait()
    turned = x_land[...].T
    for half in range(2):
        rows = pl.ds(pl.multiple_of((place[0] ^ half) * 128, 128), 128)
        x_high[rows, :], x_low[rows, :] = split(turned[half * 128 : half * 128 + 128])
    for k in range(6):
        load(k).wait()
        f_high, f_low = split(jnp.concatenate([land[2 * k], land[2 * k + 1]], axis=1))
        out = dot3(x_high[...], x_low[...], f_high, f_low, ((1,), (0,)))
        own[:, k * 256 : k * 256 + 256] = out[:128]
        other[:, k * 256 : k * 256 + 256] = out[128:]


def project(place, field, basis):
    out = jax.ShapeDtypeStruct((128, 1536), F32)
    return pl.pallas_call(
        project_kernel,
        in_specs=[pl.BlockSpec(memory_space=pltpu.SMEM)] + [pl.BlockSpec(memory_space=pl.ANY)] * 2,
        out_specs=[pl.BlockSpec(memory_space=pltpu.VMEM)] * 2,
        out_shape=[out, out],
        scratch_shapes=[
            pltpu.VMEM((12, 1024, 128), F32),
            pltpu.VMEM((1024, 256), F32),
            pltpu.VMEM((256, 1024), BF16),
            pltpu.VMEM((256, 1024), BF16),
            pltpu.SemaphoreType.DMA((7,)),
        ],
        compiler_params=pltpu.CompilerParams(vmem_limit_bytes=VMEM_LIMIT),
        cost_estimate=pl.CostEstimate(flops=2400000000, bytes_accessed=9000000, transcendentals=0),
        name="project",
    )(place, field, basis)


def send_out(place, buf, b, lane_of, g, refs, sems):
    a_refs, b_refs, c_refs = refs[0:4], refs[4:8], refs[8:12]
    dy = lax.rem((b - place[2] + 4) * place[4], 4)

    def piece(x, row, rows, third):
        row = pl.multiple_of(x * 64 + row, 16)
        return buf.at[pl.ds(row, rows), pl.ds(pl.multiple_of(lane_of(x) + third * 384, 128), 384)]

    wide, thin = pl.ds(g * 64, 64), pl.ds(g * 16, 16)
    for dx in range(4):
        x = ahead(place, 1, dx)
        pltpu.make_async_copy(piece(x, 0, 64, 0), a_refs[dx].at[b, wide], sems.at[dx]).start()
    for d in range(4):

        @pl.when(dy == d)
        def _():
            for x in range(4):
                pltpu.make_async_copy(piece(x, 0, 64, 1), b_refs[d].at[x, wide], sems.at[4 + d]).start()

        z = ahead(place, 3, d)
        for x in range(4):
            pltpu.make_async_copy(piece(x, z * 16, 16, 2), c_refs[d].at[b * 4 + x, thin], sems.at[8 + d]).start()


def wait_out(g, refs, sems):
    for i, ref in enumerate(refs):
        part = ref.at[:, pl.ds(g * 64, 64)] if i < 8 else ref.at[:, pl.ds(g * 16, 16)]
        pltpu.make_async_copy(part, part, sems.at[i]).wait()


def core_copies(place, buf, refs, sems):
    copies = []
    for d in range(4):
        for other in range(4):
            for half in range(2):
                rows = pl.ds(128 + half * 16, 16)
                q = pl.multiple_of((other * 4 + ahead(place, 1, d)) * 16, 16)
                src = buf.at[pl.ds(q, 16), pl.ds(half * 384, 384)]
                copies.append(pltpu.make_async_copy(src, refs[d].at[other, rows], sems.at[d]))
                q = pl.multiple_of((ahead(place, 2, d) * 4 + other) * 16, 16)
                src = buf.at[pl.ds(q, 16), pl.ds(768 + half * 384, 384)]
                copies.append(pltpu.make_async_copy(src, refs[4 + d].at[other, rows], sems.at[4 + d]))
    return copies


def gram_x_kernel(place, own, other, reduced, y_basis, *refs):
    high, low, buf, land, core, out_sems, sems, core_sems = refs[12:]

    def load(k):
        src = own if k < 6 else other
        part = pl.ds(k % 6 * 2, 2)
        return pltpu.make_async_copy(src.at[part], land.at[pl.ds(k * 2, 2)], sems.at[k])

    def prepare(half):
        for k in range(half * 6, half * 6 + 6):
            load(k).wait()
            for s in range(2):
                v_high, v_low = split(land[k * 2 + s])
                lane = (k % 6 * 2 + s) * 128
                high[half * 1024 : half * 1024 + 1024, lane : lane + 128] = v_high
                low[half * 1024 : half * 1024 + 1024, lane : lane + 128] = v_low

    def multiply(b, start, stop):
        rows, cols = slice(b * 256, b * 256 + 256), slice(start, stop)
        buf[b, :, start - b * 256 : stop - b * 256] = dot3(
            high[rows, :], low[rows, :], high[cols, :], low[cols, :], ((1,), (1,))
        )

    for k in range(12):
        load(k).start()
    y_high, y_low = split(y_basis[...].T)
    for s in range(12):
        r_high, r_low = split(reduced[:, s * 128 : s * 128 + 128])
        core[:, s * 128 : s * 128 + 128] = dot3(y_high, y_low, r_high, r_low, ((1,), (1,)))
    for copy in core_copies(place, core, refs, core_sems):
        copy.start()
    prepare(0)
    for b in range(4):
        multiply(b, b * 256, 1024)
    prepare(1)
    for b in range(4):
        multiply(b, 1024, b * 256 + 1280)
        send_out(place, buf.at[b], b, lambda x: (x // 2) * 128, 0, refs, out_sems)
    wait_out(0, refs[:12], out_sems)
    for i in range(8):
        part = refs[i].at[:, pl.ds(128, 32)]
        pltpu.make_async_copy(part, part, core_sems.at[i]).wait()


def gram_y_kernel(place, own, other, *refs):
    refs = refs[12:]
    high, low, buf, out_sems = refs[12:]
    for j in range(16):
        tiles = [src[j, :, s * 128 : s * 128 + 128] for src in (own, other) for s in range(12)]
        v = jnp.concatenate(tiles + [jnp.zeros((64, 128), F32)], axis=0).T
        v_high, v_low = split(v)
        for start in (j * 128, 2048 + j * 128):
            if start < 3072:
                high[start : start + 128, :] = v_high
                low[start : start + 128, :] = v_low
    h = place[0]
    for b in range(4):
        starts = [pl.multiple_of((b * 4 + x) * 128 + h * 64, 64) for x in range(4)]
        l_high = jnp.concatenate([high[pl.ds(r, 64), :] for r in starts], axis=0)
        l_low = jnp.concatenate([low[pl.ds(r, 64), :] for r in starts], axis=0)
        cols = slice(b * 512, b * 512 + 1536)
        buf[b] = dot3(l_high, l_low, high[cols, :], low[cols, :], ((1,), (1,)))
        send_out(place, buf.at[b], b, lambda x: x * 128, 1, refs, out_sems)
    wait_out(1, refs[:12], out_sems)


def gram_pieces(kernel, name, place, pieces, args, spaces, scratch, flops):
    ab = jax.ShapeDtypeStruct((4, 160, 384), F32)
    c = jax.ShapeDtypeStruct((16, 32, 384), F32)
    anywhere = pl.BlockSpec(memory_space=pl.ANY)
    return pl.pallas_call(
        kernel,
        in_specs=[pl.BlockSpec(memory_space=pltpu.SMEM)]
        + [pl.BlockSpec(memory_space=space) for space in spaces]
        + [anywhere] * len(pieces),
        out_specs=[anywhere] * 12,
        out_shape=[ab] * 8 + [c] * 4,
        scratch_shapes=scratch,
        input_output_aliases={1 + len(args) + i: i for i in range(len(pieces))},
        compiler_params=pltpu.CompilerParams(vmem_limit_bytes=VMEM_LIMIT),
        cost_estimate=pl.CostEstimate(flops=flops, bytes_accessed=20000000, transcendentals=0),
        name=name,
    )(place, *args, *pieces)


GRAM_X_SCRATCH = [
    pltpu.VMEM((2048, 1536), BF16),
    pltpu.VMEM((2048, 1536), BF16),
    pltpu.VMEM((4, 256, 1280), F32),
    pltpu.VMEM((24, 1024, 128), F32),
    pltpu.VMEM((256, 1536), F32),
    pltpu.SemaphoreType.DMA((12,)),
    pltpu.SemaphoreType.DMA((12,)),
    pltpu.SemaphoreType.DMA((8,)),
]
GRAM_Y_SCRATCH = [
    pltpu.VMEM((3072, 256), BF16),
    pltpu.VMEM((3072, 256), BF16),
    pltpu.VMEM((4, 256, 1536), F32),
    pltpu.SemaphoreType.DMA((12,)),
]


def sum4(terms, index):
    return (terms[0][index] + terms[1][index]) + (terms[2][index] + terms[3][index])


def sum_first_kernel(place, *refs):
    step = pl.program_id(0)
    a, b, c, outs = refs[0:4], refs[4:8], refs[8:12], refs[12:]
    total = sum4(a, 0)
    for d in range(4):

        @pl.when(step == d)
        def _():
            outs[d][...] = total

        z = ahead(place, 3, d)
        for g in range(2):
            rows = pl.ds(pl.multiple_of(g * 64 + z * 16, 16), 16)
            outs[4 + d][step, g * 16 : g * 16 + 16, :] = sum4(b, (0, rows, slice(None)))
        outs[8 + d][step] = sum4(c, ahead(place, 1, d))
    outs[12][step] = sum4(b, (0, slice(128, 160), slice(None)))


def sum_first(place, a, b, c):
    def whole(shape):
        return pl.BlockSpec(shape, lambda i, place: (0,) * len(shape))

    shapes = [(160, 384)] * 4 + [(4, 32, 384)] * 9
    return pl.pallas_call(
        sum_first_kernel,
        grid_spec=pltpu.PrefetchScalarGridSpec(
            num_scalar_prefetch=1,
            grid=(4,),
            in_specs=[pl.BlockSpec((1, 160, 384), lambda i, place: (ahead(place, 2, i), 0, 0))] * 4
            + [pl.BlockSpec((1, 160, 384), lambda i, place: (i, 0, 0))] * 4
            + [pl.BlockSpec((4, 32, 384), lambda i, place: (i, 0, 0))] * 4,
            out_specs=[whole(shape) for shape in shapes],
        ),
        out_shape=[jax.ShapeDtypeStruct(shape, F32) for shape in shapes],
        compiler_params=pltpu.CompilerParams(vmem_limit_bytes=VMEM_LIMIT),
        cost_estimate=pl.CostEstimate(flops=3000000, bytes_accessed=14000000, transcendentals=0),
        name="sum_first",
    )(place, *a, *b, *c)


def sum_second_kernel(place, *refs):
    a, b, c, b_core, outs = refs[0:4], refs[4:8], refs[8:12], refs[12], refs[13:]
    for d in range(4):
        for g in range(2):
            rows = pl.ds(pl.multiple_of(g * 64 + ahead(place, 3, d) * 16, 16), 16)
            outs[d][g * 16 : g * 16 + 16, :] = sum4(a, (rows, slice(None)))
        x = ahead(place, 1, d)
        outs[4 + d][:32, :] = sum4(b, x)
        outs[4 + d][32:, :] = b_core[x]
        outs[8 + d][...] = sum4(c, ahead(place, 2, d))
    outs[12][...] = sum4(a, (slice(128, 160), slice(None)))


def sum_last_kernel(place, *refs):
    a, b, c, a_core = refs[0:4], refs[4:8], refs[8:12], refs[12]
    slots, direct_x, keep, give, core, wide = refs[13:]
    h = place[0]
    j = place[2] * 4 + place[1]
    block_x = h * 8 + j // 2
    core[:32, :] = a_core[...]
    core[32:, :] = sum4(b, (slice(32, 64), slice(None)))
    parts = [sum4(t, (slice(0, 32), slice(None))) for t in (a, b, c)]
    zero = jnp.zeros((16, 128), F32)
    for k in range(16):
        lane = k % 3 * 128
        tile_x = parts[k // 3][:16, lane : lane + 128] if k < 9 else zero
        tile_y = parts[k // 3][16:, lane : lane + 128] if k < 9 else zero
        to_x, to_y = lax.rem(block_x + k, 16), lax.rem(j + k, 16)
        direct_x[to_x] = tile_x
        wide[lax.rem(to_y + 8 * h, 16)] = tile_y
        slots[2 * to_x, 0] = tile_x
        slots[2 * to_x + 1, 0] = tile_x
        slots[to_y, 1] = tile_y
        slots[16 + to_y, 1] = tile_y
    keep[...] = wide[:8]
    give[...] = wide[8:]


def select_kernel(place, got, direct_x, keep, come, out):
    h = place[0]
    j = place[2] * 4 + place[1]
    block_x = h * 8 + j // 2
    for block in range(16):
        first, second = got[2 * block, 0], got[2 * block + 1, 0]
        even = jnp.concatenate([first[:, :64], second[:, :64]], axis=1)
        odd = jnp.concatenate([first[:, 64:], second[:, 64:]], axis=1)
        turned = jnp.where(lax.rem(j, 2) == 0, even, odd)
        out[block] = jnp.where(lax.rem(block - block_x + 16, 16) <= 8, direct_x[block], turned)
    for block in range(8):
        is_direct = lax.rem(h * 8 + block - j + 16, 16) <= 8
        for half in range(2):
            direct = jnp.where(h == half, keep[block], come[block])
            out[16 + 2 * block + half] = jnp.where(is_direct, direct, got[half * 16 + h * 8 + block, 1])


def assemble_kernel(scale_x, scale_y, place, q0, q1, q2, q3, gram_x, gram_y, rows):
    h = place[0]
    j = place[2] * 4 + place[1]
    block_x = h * 8 + j // 2
    for d, quarter in enumerate((q0, q1, q2, q3)):
        z = ahead(place, 3, 4 - d)
        rows[:, pl.ds(pl.multiple_of(z * 16, 16), 16), :] = quarter[...]
    for block in range(16):
        direct = rows[block]
        turned = direct.T
        turned = jnp.concatenate([turned[:64], turned[64:]], axis=1)
        is_direct = lax.rem(block - block_x + 16, 16) <= 8
        gram_x[:, block * 128 : block * 128 + 128] = jnp.where(is_direct, direct, turned) * scale_x
    for block in range(8):
        direct = jnp.concatenate([rows[16 + 2 * block], rows[17 + 2 * block]], axis=0)
        is_direct = lax.rem(h * 8 + block - j + 16, 16) <= 8
        gram_y[:, block * 128 : block * 128 + 128] = jnp.where(is_direct, direct, direct.T) * scale_y


def small_kernel(kernel, name, out_shape, scratch, *args):
    return pl.pallas_call(
        kernel,
        in_specs=[pl.BlockSpec(memory_space=pltpu.SMEM)] + [pl.BlockSpec(memory_space=pltpu.VMEM)] * (len(args) - 1),
        out_shape=out_shape,
        scratch_shapes=scratch,
        compiler_params=pltpu.CompilerParams(vmem_limit_bytes=VMEM_LIMIT),
        name=name,
    )(*args)


def per_device(species_field, x_mode_basis, y_mode_basis):
    h, j, z0 = lax.axis_index("gx"), lax.axis_index("gy"), lax.axis_index("gz")
    x0, y0 = j % 4, j // 4
    place = jnp.stack([h, x0, y0, z0, 1 + 2 * h]).astype(jnp.int32)
    nx = 2 * species_field.shape[1]
    ny = 16 * species_field.shape[2]
    slices = 4 * species_field.shape[0]
    ranks = x_mode_basis.shape[1]

    other_field = lax.ppermute(species_field, "gx", SWAP)
    mine, theirs = project(place, species_field, x_mode_basis)
    reduced = mine + lax.ppermute(theirs, "gx", SWAP)
    fibers = lax.all_to_all(reduced.reshape(16, 8, 1536), "gy", 0, 0, tiled=True)

    pieces = gram_pieces(
        gram_x_kernel, "gram_x", place, [], (species_field, other_field, reduced, y_mode_basis),
        (pl.ANY, pl.ANY, pltpu.VMEM, pltpu.VMEM), GRAM_X_SCRATCH, 12000000000,
    )
    pieces, fibers = lax.optimization_barrier((pieces, fibers))
    other_fibers = lax.ppermute(fibers, "gx", SWAP)
    pieces = gram_pieces(
        gram_y_kernel, "gram_y", place, pieces, (fibers, other_fibers), (pltpu.VMEM, pltpu.VMEM), GRAM_Y_SCRATCH, 2400000000
    )

    def stage(a, b, c, shifts):
        def send(terms, d):
            return [shift(t, d) for shift, t in zip(shifts, terms)]

        near = [send([a[d], b[d], c[d]], d) for d in (1, 3)]
        far, near[0] = lax.optimization_barrier(([a[2], b[2], c[2]], near[0]))
        came = lax.optimization_barrier(near + [send(far, 2)])
        return [[own[0]] + [t[i] for t in came] for i, own in enumerate((a, b, c))]

    a, b, c = stage(pieces[0:4], pieces[4:8], pieces[8:12], (shift_x, shift_y, shift_z))
    *sums, b_core = sum_first(place, a, b, c)
    a, b, c = stage(sums[0:4], sums[4:8], sums[8:12], (shift_y, shift_z, shift_x))
    small, wide = jax.ShapeDtypeStruct((32, 384), F32), jax.ShapeDtypeStruct((64, 384), F32)
    *sums, a_core = small_kernel(
        sum_second_kernel, "sum_second", [small] * 4 + [wide] * 4 + [small] * 5, [], place, *a, *b, *c, b_core
    )
    a, b, c = stage(sums[0:4], sums[4:8], sums[8:12], (shift_z, shift_x, shift_y))
    blocks = jax.ShapeDtypeStruct((8, 16, 128), F32)
    slots, direct_x, keep, give, core = small_kernel(
        sum_last_kernel, "sum_last",
        [jax.ShapeDtypeStruct((32, 2, 16, 128), F32), jax.ShapeDtypeStruct((16, 16, 128), F32), blocks, blocks, wide],
        [pltpu.VMEM((16, 16, 128), F32)],
        place, *a, *b, *c, a_core,
    )
    core = core.reshape(2, 2, 16, 3, 128).transpose(4, 0, 1, 3, 2).reshape(128, 12, 16)

    got = lax.all_to_all(slots, ("gx", "gy"), 0, 0, tiled=True)
    come = lax.ppermute(give, "gx", SWAP)
    part = small_kernel(
        select_kernel, "select", jax.ShapeDtypeStruct((32, 16, 128), F32), [], place, got, direct_x, keep, come
    )
    quarters = [part] + [shift_z(part, d) for d in (1, 2, 3)]
    gram_x, gram_y = small_kernel(
        functools.partial(assemble_kernel, 1.0 / (ny * slices), 1.0 / (ranks * slices)),
        "assemble",
        [jax.ShapeDtypeStruct((64, nx), F32), jax.ShapeDtypeStruct((128, ny // 2), F32)],
        [pltpu.VMEM((32, 64, 128), F32)],
        place, *quarters,
    )
    return (gram_x, gram_y, core)


def solution(mesh):
    in_specs = (P("gz", "gx", "gy"), P("gx", None), P("gy", None))
    out_specs = (P(("gx", "gy"), None), P("gy", "gx"), P("gx", "gz", "gy"))
    return jax.shard_map(
        per_device, mesh=mesh, in_specs=in_specs, out_specs=out_specs, check_vma=False
    )
```

```python
import functools

import jax
import jax.numpy as jnp
from jax import lax
from jax.experimental import pallas as pl
from jax.experimental.pallas import tpu as pltpu
from jax.sharding import PartitionSpec as P

F32 = jnp.float32
BF16 = jnp.bfloat16
VMEM_LIMIT = 58 * 1024 * 1024

SWAP = [(0, 1), (1, 0)]


def device(h, y, x, z):
    return (h * 16 + y % 4 * 4 + x % 4) * 4 + z % 4


def stepper(axis):
    def step(v, d):
        pairs = []
        for h in range(2):
            by = d if h == 0 else -d
            move = [by if name == axis else 0 for name in "yxz"]
            for y in range(4):
                for x in range(4):
                    for z in range(4):
                        pairs.append((device(h, y, x, z), device(h, y + move[0], x + move[1], z + move[2])))
        return lax.ppermute(v, ("gx", "gy", "gz"), pairs)

    return step


shift_x, shift_y, shift_z = stepper("x"), stepper("y"), stepper("z")


def swapper(axis):
    def swap(v, turn):
        pairs = []
        for h in range(2):
            mask = 1 if h == turn else 3
            for y in range(4):
                for x in range(4):
                    for z in range(4):
                        to = [c ^ mask if name == axis else c for name, c in zip("yxz", (y, x, z))]
                        pairs.append((device(h, y, x, z), device(h, *to)))
        return lax.ppermute(v, ("gx", "gy", "gz"), pairs)

    return swap


swap_x, swap_y, swap_z = swapper("x"), swapper("y"), swapper("z")


def ahead(place, axis, d):
    return lax.rem(place[axis] + d * place[4], 4)


def owner_masks(place):
    return ((0, 0, 0), (1, 0, place[4]), (1, 1, 2), (0, 1, 4 - place[4]))


def split(v):
    high = v.astype(BF16)
    return high, (v - high.astype(F32)).astype(BF16)


def dot3(a_high, a_low, b_high, b_low, dims):
    dot = functools.partial(lax.dot_general, dimension_numbers=(dims, ((), ())), preferred_element_type=F32)
    return dot(a_high, b_high) + (dot(a_high, b_low) + dot(a_low, b_high))


def project_kernel(place, field, basis, own, other, land, x_land, x_high, x_low, f_high, f_low, sems):
    def load(k):
        part = pl.ds(k * 2, 2)
        return pltpu.make_async_copy(field.at[part], land.at[part], sems.at[k])

    x_load = pltpu.make_async_copy(basis, x_land, sems.at[6])
    x_load.start()
    for k in range(6):
        load(k).start()
    x_load.wait()
    turned = x_land[...].T
    for half in range(2):
        rows = pl.ds(pl.multiple_of((place[0] ^ half) * 128, 128), 128)
        x_high[rows, :], x_low[rows, :] = split(turned[half * 128 : half * 128 + 128])
    for k in range(6):
        load(k).wait()
        for s in (2 * k, 2 * k + 1):
            f_high[:, s * 128 : s * 128 + 128], f_low[:, s * 128 : s * 128 + 128] = split(land[s])
    out = dot3(x_high[...], x_low[...], f_high[...], f_low[...], ((1,), (0,)))
    own[...] = out[:128]
    other[...] = out[128:]


def project(place, field, basis):
    out = jax.ShapeDtypeStruct((128, 1536), F32)
    return pl.pallas_call(
        project_kernel,
        in_specs=[pl.BlockSpec(memory_space=pltpu.SMEM)] + [pl.BlockSpec(memory_space=pl.ANY)] * 2,
        out_specs=[pl.BlockSpec(memory_space=pltpu.VMEM)] * 2,
        out_shape=[out, out],
        scratch_shapes=[
            pltpu.VMEM((12, 1024, 128), F32),
            pltpu.VMEM((1024, 256), F32),
            pltpu.VMEM((256, 1024), BF16),
            pltpu.VMEM((256, 1024), BF16),
            pltpu.VMEM((1024, 1536), BF16),
            pltpu.VMEM((1024, 1536), BF16),
            pltpu.SemaphoreType.DMA((7,)),
        ],
        compiler_params=pltpu.CompilerParams(vmem_limit_bytes=VMEM_LIMIT),
        cost_estimate=pl.CostEstimate(flops=2400000000, bytes_accessed=9000000, transcendentals=0),
        name="project",
    )(place, field, basis)


def send_out(place, buf, b, lane_of, refs, sems):
    def piece(x, row, rows, third):
        row = pl.multiple_of(x * 64 + row, 16)
        return buf.at[pl.ds(row, rows), pl.ds(pl.multiple_of(lane_of(x) + third * 384, 128), 384)]

    rows = pl.ds(0, 64)
    for sent, slot, mask in owner_masks(place):
        x, z = place[1] ^ mask, place[3] ^ mask
        pltpu.make_async_copy(piece(x, 0, 64, 0), refs[sent].at[slot, b, rows], sems.at[sent]).start()

        @pl.when(place[2] ^ mask == b)
        def _():
            for x in range(4):
                pltpu.make_async_copy(piece(x, 0, 64, 1), refs[2 + sent].at[slot, x, rows], sems.at[2 + sent]).start()

        for x in range(4):
            to = refs[4 + sent].at[slot, b * 4 + x]
            pltpu.make_async_copy(piece(x, z * 16, 16, 2), to, sems.at[4 + sent]).start()


def wait_out(refs, sems):
    for i, ref in enumerate(refs):
        part = ref.at[:, :, pl.ds(0, 64)] if i < 4 else ref
        pltpu.make_async_copy(part, part, sems.at[i]).wait()


def core_copies(place, buf, refs, sems):
    copies = []
    for sent, slot, mask in owner_masks(place):
        for other in range(4):
            for half in range(2):
                rows = pl.ds(64 + half * 16, 16)
                q = pl.multiple_of((other * 4 + (place[1] ^ mask)) * 16, 16)
                src = buf.at[pl.ds(q, 16), pl.ds(half * 384, 384)]
                copies.append(pltpu.make_async_copy(src, refs[sent].at[slot, other, rows], sems.at[sent]))
                q = pl.multiple_of(((place[2] ^ mask) * 4 + other) * 16, 16)
                src = buf.at[pl.ds(q, 16), pl.ds(768 + half * 384, 384)]
                copies.append(pltpu.make_async_copy(src, refs[2 + sent].at[slot, other, rows], sems.at[2 + sent]))
    return copies


def gram_x_kernel(place, own, other, reduced, y_basis, *refs):
    high, low, buf, land, core, out_sems, sems, core_sems = refs[6:]

    def load(k):
        src = own if k < 6 else other
        part = pl.ds(k % 6 * 2, 2)
        return pltpu.make_async_copy(src.at[part], land.at[pl.ds(k * 2, 2)], sems.at[k])

    for k in range(12):
        load(k).start()
    y_high, y_low = split(y_basis[...].T)
    for s in range(12):
        r_high, r_low = split(reduced[:, s * 128 : s * 128 + 128])
        core[:, s * 128 : s * 128 + 128] = dot3(y_high, y_low, r_high, r_low, ((1,), (1,)))
    for copy in core_copies(place, core, refs, core_sems):
        copy.start()
    for k in range(12):
        load(k).wait()
        for s in (2 * k, 2 * k + 1):
            rows, cols = slice(s // 12 * 1024, s // 12 * 1024 + 1024), slice(s % 12 * 128, s % 12 * 128 + 128)
            high[rows, cols], low[rows, cols] = split(land[s])
    for b in range(4):
        rows, cols = slice(b * 256, b * 256 + 256), slice(b * 256, b * 256 + 1280)
        buf[b] = dot3(high[rows, :], low[rows, :], high[cols, :], low[cols, :], ((1,), (1,)))
        send_out(place, buf.at[b], b, lambda x: (x // 2) * 128, refs, out_sems)
    wait_out(refs[:6], out_sems)
    for i in range(4):
        part = refs[i].at[:, :, pl.ds(64, 32)]
        pltpu.make_async_copy(part, part, core_sems.at[i]).wait()


def gram_y_kernel(place, own, other, *refs):
    high, low, buf, out_sems = refs[6:]
    for j in range(16):
        tiles = [src[j, :, s * 128 : s * 128 + 128] for src in (own, other) for s in range(12)]
        v = jnp.concatenate(tiles + [jnp.zeros((64, 128), F32)], axis=0).T
        v_high, v_low = split(v)
        for start in (j * 128, 2048 + j * 128):
            if start < 3072:
                high[start : start + 128, :] = v_high
                low[start : start + 128, :] = v_low
    h = place[0]
    for b in range(4):
        starts = [pl.multiple_of((b * 4 + x) * 128 + h * 64, 64) for x in range(4)]
        l_high = jnp.concatenate([high[pl.ds(r, 64), :] for r in starts], axis=0)
        l_low = jnp.concatenate([low[pl.ds(r, 64), :] for r in starts], axis=0)
        cols = slice(b * 512, b * 512 + 1536)
        buf[b] = dot3(l_high, l_low, high[cols, :], low[cols, :], ((1,), (1,)))
        send_out(place, buf.at[b], b, lambda x: x * 128, refs, out_sems)
    wait_out(refs[:6], out_sems)


def gram_pieces(kernel, name, rows, place, args, spaces, scratch, flops):
    ab = jax.ShapeDtypeStruct((2, 4, rows, 384), F32)
    c = jax.ShapeDtypeStruct((2, 16, 16, 384), F32)
    return pl.pallas_call(
        kernel,
        in_specs=[pl.BlockSpec(memory_space=space) for space in (pltpu.SMEM,) + spaces],
        out_specs=[pl.BlockSpec(memory_space=pl.ANY)] * 6,
        out_shape=[ab] * 4 + [c] * 2,
        scratch_shapes=scratch,
        compiler_params=pltpu.CompilerParams(vmem_limit_bytes=VMEM_LIMIT),
        cost_estimate=pl.CostEstimate(flops=flops, bytes_accessed=20000000, transcendentals=0),
        name=name,
    )(place, *args)


GRAM_X_SCRATCH = [
    pltpu.VMEM((2048, 1536), BF16),
    pltpu.VMEM((2048, 1536), BF16),
    pltpu.VMEM((4, 256, 1280), F32),
    pltpu.VMEM((24, 1024, 128), F32),
    pltpu.VMEM((256, 1536), F32),
    pltpu.SemaphoreType.DMA((6,)),
    pltpu.SemaphoreType.DMA((12,)),
    pltpu.SemaphoreType.DMA((4,)),
]
GRAM_Y_SCRATCH = [
    pltpu.VMEM((3072, 256), BF16),
    pltpu.VMEM((3072, 256), BF16),
    pltpu.VMEM((4, 256, 1536), F32),
    pltpu.SemaphoreType.DMA((12,)),
]


def sum4(terms, index):
    return (terms[0][index] + terms[1][index]) + (terms[2][index] + terms[3][index])


def add_kernel(*refs):
    *terms, out = refs
    at = 0
    for kept, came in zip(terms[0::2], terms[1::2]):
        rows = kept.shape[2]
        out[:, at : at + rows, :] = kept[0] + came[0]
        at += rows


def slab_of(v, k):
    return pl.BlockSpec((1,) + v.shape[1:], lambda i: (k, 0, 0, 0))


def add_for_second(terms):
    shape = (terms[0].shape[1], sum(v.shape[2] for v in terms[0::2]), 384)
    return pl.pallas_call(
        add_kernel,
        grid=(1,),
        in_specs=[slab_of(v, 1) for v in terms],
        out_specs=pl.BlockSpec(shape, lambda i: (0, 0, 0)),
        out_shape=jax.ShapeDtypeStruct(shape, F32),
        compiler_params=pltpu.CompilerParams(vmem_limit_bytes=VMEM_LIMIT),
        cost_estimate=pl.CostEstimate(flops=200000, bytes_accessed=3000000, transcendentals=0),
        name="add",
    )(*terms)


def sum_first_kernel(axis, place, *refs):
    terms, last, outs = refs[:4], refs[4], refs[5:]
    at = 0
    for kept, came in zip(terms[0::2], terms[1::2]):
        rows = slice(at, at + kept.shape[2])
        if axis is None:
            outs[0][:, rows, :] = (kept[0] + came[0]) + last[:, rows, :]
        else:
            for d, out in enumerate(outs):
                k = ahead(place, axis, d)
                out[rows, :] = (kept[0, k] + came[0, k]) + last[k, rows, :]
        at = rows.stop


def sum_first(place, axis, terms, last):
    shapes = [last.shape] if axis is None else [last.shape[1:]] * 4
    return pl.pallas_call(
        functools.partial(sum_first_kernel, axis),
        grid=(1,),
        in_specs=[pl.BlockSpec(memory_space=pltpu.SMEM)]
        + [slab_of(v, 0) for v in terms]
        + [pl.BlockSpec(last.shape, lambda i: (0, 0, 0))],
        out_specs=[pl.BlockSpec(out, lambda i, n=len(out): (0,) * n) for out in shapes],
        out_shape=[jax.ShapeDtypeStruct(out, F32) for out in shapes],
        compiler_params=pltpu.CompilerParams(vmem_limit_bytes=VMEM_LIMIT),
        cost_estimate=pl.CostEstimate(flops=1000000, bytes_accessed=4000000, transcendentals=0),
        name="sum_first",
    )(place, *terms, last)


def sum_second_kernel(place, *refs):
    outs = refs[8:]
    for part in range(2):
        terms = refs[part * 4 : part * 4 + 4]
        for d in range(4):
            for g in range(2):
                rows = pl.ds(pl.multiple_of(g * 96 + ahead(place, 3, d) * 16, 16), 16)
                to = part * 32 + g * 16
                outs[d][to : to + 16, :] = sum4(terms, (rows, slice(None)))
        outs[4][part * 32 : part * 32 + 32, :] = sum4(terms, (slice(64, 96), slice(None)))


def sum_last_kernel(place, *refs):
    slots, direct_x, keep, give, wide = refs[5:]
    h = place[0]
    j = place[2] * 4 + place[1]
    block_x = h * 8 + j // 2
    parts = [sum4(refs[:4], (slice(0, 32), slice(None))), sum4(refs[:4], (slice(32, 64), slice(None))), refs[4][...]]
    zero = jnp.zeros((16, 128), F32)
    for k in range(16):
        lane = k % 3 * 128
        tile_x = parts[k // 3][:16, lane : lane + 128] if k < 9 else zero
        tile_y = parts[k // 3][16:, lane : lane + 128] if k < 9 else zero
        to_x, to_y = lax.rem(block_x + k, 16), lax.rem(j + k, 16)
        direct_x[to_x] = tile_x
        wide[lax.rem(to_y + 8 * h, 16)] = tile_y
        slots[2 * to_x, 0] = tile_x
        slots[2 * to_x + 1, 0] = tile_x
        slots[to_y, 1] = tile_y
        slots[16 + to_y, 1] = tile_y
    keep[...] = wide[:8]
    give[...] = wide[8:]


def select_kernel(place, got, direct_x, keep, come, out):
    h = place[0]
    j = place[2] * 4 + place[1]
    block_x = h * 8 + j // 2
    for block in range(16):
        first, second = got[2 * block, 0], got[2 * block + 1, 0]
        even = jnp.concatenate([first[:, :64], second[:, :64]], axis=1)
        odd = jnp.concatenate([first[:, 64:], second[:, 64:]], axis=1)
        turned = jnp.where(lax.rem(j, 2) == 0, even, odd)
        out[block] = jnp.where(lax.rem(block - block_x + 16, 16) <= 8, direct_x[block], turned)
    for block in range(8):
        is_direct = lax.rem(h * 8 + block - j + 16, 16) <= 8
        for half in range(2):
            direct = jnp.where(h == half, keep[block], come[block])
            out[16 + 2 * block + half] = jnp.where(is_direct, direct, got[half * 16 + h * 8 + block, 1])


def assemble_kernel(scale_x, scale_y, place, q0, q1, q2, q3, gram_x, gram_y, rows):
    h = place[0]
    j = place[2] * 4 + place[1]
    block_x = h * 8 + j // 2
    for d, quarter in enumerate((q0, q1, q2, q3)):
        z = ahead(place, 3, 4 - d)
        rows[:, pl.ds(pl.multiple_of(z * 16, 16), 16), :] = quarter[...]
    for block in range(16):
        direct = rows[block]
        turned = direct.T
        turned = jnp.concatenate([turned[:64], turned[64:]], axis=1)
        is_direct = lax.rem(block - block_x + 16, 16) <= 8
        gram_x[:, block * 128 : block * 128 + 128] = jnp.where(is_direct, direct, turned) * scale_x
    for block in range(8):
        direct = jnp.concatenate([rows[16 + 2 * block], rows[17 + 2 * block]], axis=0)
        is_direct = lax.rem(h * 8 + block - j + 16, 16) <= 8
        gram_y[:, block * 128 : block * 128 + 128] = jnp.where(is_direct, direct, direct.T) * scale_y


def add_two_kernel(place, first, second, out):
    out[...] = first[...] + second[...]


def small_kernel(kernel, name, out_shape, scratch, *args):
    return pl.pallas_call(
        kernel,
        in_specs=[pl.BlockSpec(memory_space=pltpu.SMEM)] + [pl.BlockSpec(memory_space=pltpu.VMEM)] * (len(args) - 1),
        out_shape=out_shape,
        scratch_shapes=scratch,
        compiler_params=pltpu.CompilerParams(vmem_limit_bytes=VMEM_LIMIT),
        name=name,
    )(*args)


def per_device(species_field, x_mode_basis, y_mode_basis):
    h, j, z0 = lax.axis_index("gx"), lax.axis_index("gy"), lax.axis_index("gz")
    x0, y0 = j % 4, j // 4
    place = jnp.stack([h, x0, y0, z0, 1 + 2 * h]).astype(jnp.int32)
    nx = 2 * species_field.shape[1]
    ny = 16 * species_field.shape[2]
    slices = 4 * species_field.shape[0]
    ranks = x_mode_basis.shape[1]

    other_field = lax.ppermute(species_field, "gx", SWAP)
    mine, theirs = project(place, species_field, x_mode_basis)
    reduced = small_kernel(
        add_two_kernel, "add_two", jax.ShapeDtypeStruct((128, 1536), F32), [], place, mine, lax.ppermute(theirs, "gx", SWAP)
    )
    fibers = lax.all_to_all(reduced.reshape(16, 8, 1536), "gy", 0, 0, tiled=True)

    def first_swaps(pieces):
        return [swap(pieces[2 * i + 1], 0) for i, swap in enumerate((swap_x, swap_y, swap_z))]

    px = gram_pieces(
        gram_x_kernel, "gram_x", 96, place, (species_field, other_field, reduced, y_mode_basis),
        (pl.ANY, pl.ANY, pltpu.VMEM, pltpu.VMEM), GRAM_X_SCRATCH, 12000000000,
    )
    px, fibers = lax.optimization_barrier((px, fibers))
    other_fibers = lax.ppermute(fibers, "gx", SWAP)
    came_x = first_swaps(px)
    py = gram_pieces(
        gram_y_kernel, "gram_y", 64, place, (fibers, other_fibers), (pltpu.VMEM, pltpu.VMEM), GRAM_Y_SCRATCH, 2400000000
    )
    came_y = first_swaps(py)

    def ring(terms, shift):
        up, down = shift(terms[1], 1), shift(terms[3], 3)
        far, up = lax.optimization_barrier((terms[2], up))
        return [terms[0], up, down, shift(far, 2)]

    terms_a, terms_b, terms_c = [(px[2 * i], came_x[i], py[2 * i], came_y[i]) for i in range(3)]
    add_c = add_for_second(terms_c)
    add_c, terms_a, terms_b = lax.optimization_barrier((add_c, terms_a, terms_b))
    (c,) = sum_first(place, None, terms_c, swap_z(add_c, 1))
    a = sum_first(place, 2, terms_a, swap_x(add_for_second(terms_a), 1))
    b = sum_first(place, 1, terms_b, swap_y(add_for_second(terms_b), 1))
    a, b = ring(a, shift_y), ring(b, shift_x)
    a, b, c = lax.optimization_barrier((a, b, c))
    c = lax.all_to_all(c, "gy", 0, 0, tiled=True).sum(axis=0)
    part = jax.ShapeDtypeStruct((64, 384), F32)
    *quarters, core = small_kernel(
        sum_second_kernel, "sum_second", [part] * 5, [], place, *a, *b
    )
    blocks = jax.ShapeDtypeStruct((8, 16, 128), F32)
    slots, direct_x, keep, give = small_kernel(
        sum_last_kernel, "sum_last",
        [jax.ShapeDtypeStruct((32, 2, 16, 128), F32), jax.ShapeDtypeStruct((16, 16, 128), F32), blocks, blocks],
        [pltpu.VMEM((16, 16, 128), F32)],
        place, *[quarters[0]] + [shift_z(quarters[d], d) for d in (1, 2, 3)], c,
    )
    core = core.reshape(2, 2, 16, 3, 128).transpose(4, 0, 1, 3, 2).reshape(128, 12, 16)

    got = lax.all_to_all(slots, ("gx", "gy"), 0, 0, tiled=True)
    come = lax.ppermute(give, "gx", SWAP)
    part = small_kernel(
        select_kernel, "select", jax.ShapeDtypeStruct((32, 16, 128), F32), [], place, got, direct_x, keep, come
    )
    quarters = [part] + [shift_z(part, d) for d in (1, 2, 3)]
    gram_x, gram_y = small_kernel(
        functools.partial(assemble_kernel, 1.0 / (ny * slices), 1.0 / (ranks * slices)),
        "assemble",
        [jax.ShapeDtypeStruct((64, nx), F32), jax.ShapeDtypeStruct((128, ny // 2), F32)],
        [pltpu.VMEM((32, 64, 128), F32)],
        place, *quarters,
    )
    return (gram_x, gram_y, core)


def solution(mesh):
    in_specs = (P("gz", "gx", "gy"), P("gx", None), P("gy", None))
    out_specs = (P(("gx", "gy"), None), P("gy", "gx"), P("gx", "gz", "gy"))
    return jax.shard_map(
        per_device, mesh=mesh, in_specs=in_specs, out_specs=out_specs, check_vma=False
    )
```

```python
import functools

import jax
import jax.numpy as jnp
from jax import lax
from jax.experimental import pallas as pl
from jax.experimental.pallas import tpu as pltpu
from jax.sharding import PartitionSpec as P

F32 = jnp.float32
BF16 = jnp.bfloat16
VMEM_LIMIT = 58 * 1024 * 1024

SWAP = [(0, 1), (1, 0)]


def device(h, y, x, z):
    return (h * 16 + y % 4 * 4 + x % 4) * 4 + z % 4


def stepper(axis):
    def step(v, d):
        pairs = []
        for h in range(2):
            by = d if h == 0 else -d
            move = [by if name == axis else 0 for name in "yxz"]
            for y in range(4):
                for x in range(4):
                    for z in range(4):
                        pairs.append((device(h, y, x, z), device(h, y + move[0], x + move[1], z + move[2])))
        return lax.ppermute(v, ("gx", "gy", "gz"), pairs)

    return step


shift_x, shift_y, shift_z = stepper("x"), stepper("y"), stepper("z")


def swapper(axis):
    def swap(v, turn):
        pairs = []
        for h in range(2):
            mask = 1 if h == turn else 3
            for y in range(4):
                for x in range(4):
                    for z in range(4):
                        to = [c ^ mask if name == axis else c for name, c in zip("yxz", (y, x, z))]
                        pairs.append((device(h, y, x, z), device(h, *to)))
        return lax.ppermute(v, ("gx", "gy", "gz"), pairs)

    return swap


swap_x, swap_y, swap_z = swapper("x"), swapper("y"), swapper("z")


def ahead(place, axis, d):
    return lax.rem(place[axis] + d * place[4], 4)


def owner_masks(place):
    return ((0, 0, 0), (1, 0, place[4]), (1, 1, 2), (0, 1, 4 - place[4]))


def split(v):
    high = v.astype(BF16)
    return high, (v - high.astype(F32)).astype(BF16)


def dot3(a_high, a_low, b_high, b_low, dims):
    dot = functools.partial(lax.dot_general, dimension_numbers=(dims, ((), ())), preferred_element_type=F32)
    return dot(a_high, b_high) + (dot(a_high, b_low) + dot(a_low, b_high))


def project_kernel(place, field, basis, own, other, both, land, x_land, x_high, x_low, f_high, f_low, sems):
    def load(k):
        part = pl.ds(k * 2, 2)
        return pltpu.make_async_copy(field.at[part], land.at[part], sems.at[k])

    x_load = pltpu.make_async_copy(basis, x_land, sems.at[6])
    x_load.start()
    for k in range(6):
        load(k).start()
    x_load.wait()
    turned = x_land[...].T
    for half in range(2):
        rows = pl.ds(pl.multiple_of((place[0] ^ half) * 128, 128), 128)
        x_high[rows, :], x_low[rows, :] = split(turned[half * 128 : half * 128 + 128])
    for k in range(6):
        load(k).wait()
        for s in (2 * k, 2 * k + 1):
            f_high[:, s * 128 : s * 128 + 128], f_low[:, s * 128 : s * 128 + 128] = split(land[s])
    out = dot3(x_high[...], x_low[...], f_high[...], f_low[...], ((1,), (0,)))
    own[...] = out[:128]
    other[...] = out[128:]
    for j in range(16):
        both[j, :8] = out[j * 8 : j * 8 + 8]
        both[j, 8:] = out[128 + j * 8 : 136 + j * 8]


def project(place, field, basis):
    out = jax.ShapeDtypeStruct((128, 1536), F32)
    return pl.pallas_call(
        project_kernel,
        in_specs=[pl.BlockSpec(memory_space=pltpu.SMEM)] + [pl.BlockSpec(memory_space=pl.ANY)] * 2,
        out_specs=[pl.BlockSpec(memory_space=pltpu.VMEM)] * 3,
        out_shape=[out, out, jax.ShapeDtypeStruct((16, 16, 1536), F32)],
        scratch_shapes=[
            pltpu.VMEM((12, 1024, 128), F32),
            pltpu.VMEM((1024, 256), F32),
            pltpu.VMEM((256, 1024), BF16),
            pltpu.VMEM((256, 1024), BF16),
            pltpu.VMEM((1024, 1536), BF16),
            pltpu.VMEM((1024, 1536), BF16),
            pltpu.SemaphoreType.DMA((7,)),
        ],
        compiler_params=pltpu.CompilerParams(vmem_limit_bytes=VMEM_LIMIT),
        cost_estimate=pl.CostEstimate(flops=2400000000, bytes_accessed=9000000, transcendentals=0),
        name="project",
    )(place, field, basis)


def send_out(place, buf, b, lane_of, refs, sems):
    def piece(x, row, rows, third):
        row = pl.multiple_of(x * 64 + row, 16)
        return buf.at[pl.ds(row, rows), pl.ds(pl.multiple_of(lane_of(x) + third * 384, 128), 384)]

    rows = pl.ds(0, 64)
    for sent, slot, mask in owner_masks(place):
        x, z = place[1] ^ mask, place[3] ^ mask
        pltpu.make_async_copy(piece(x, 0, 64, 0), refs[sent].at[slot, b, rows], sems.at[sent]).start()

        @pl.when(place[2] ^ mask == b)
        def _():
            for x in range(4):
                pltpu.make_async_copy(piece(x, 0, 64, 1), refs[2 + sent].at[slot, x, rows], sems.at[2 + sent]).start()

        for x in range(4):
            to = refs[4 + sent].at[slot, b * 4 + x]
            pltpu.make_async_copy(piece(x, z * 16, 16, 2), to, sems.at[4 + sent]).start()


def wait_out(refs, sems):
    for i, ref in enumerate(refs):
        part = ref.at[:, :, pl.ds(0, 64)] if i < 4 else ref
        pltpu.make_async_copy(part, part, sems.at[i]).wait()


def core_copies(place, buf, refs, sems):
    copies = []
    for sent, slot, mask in owner_masks(place):
        for other in range(4):
            for half in range(2):
                rows = pl.ds(64 + half * 16, 16)
                q = pl.multiple_of((other * 4 + (place[1] ^ mask)) * 16, 16)
                src = buf.at[pl.ds(q, 16), pl.ds(half * 384, 384)]
                copies.append(pltpu.make_async_copy(src, refs[sent].at[slot, other, rows], sems.at[sent]))
                q = pl.multiple_of(((place[2] ^ mask) * 4 + other) * 16, 16)
                src = buf.at[pl.ds(q, 16), pl.ds(768 + half * 384, 384)]
                copies.append(pltpu.make_async_copy(src, refs[2 + sent].at[slot, other, rows], sems.at[2 + sent]))
    return copies


def gram_x_kernel(place, own, other, mine, theirs, y_basis, *refs):
    high, low, buf, land, core, out_sems, sems, core_sems = refs[6:]

    def load(k):
        src = own if k < 6 else other
        part = pl.ds(k % 6 * 2, 2)
        return pltpu.make_async_copy(src.at[part], land.at[pl.ds(k * 2, 2)], sems.at[k])

    for k in range(12):
        load(k).start()
    y_high, y_low = split(y_basis[...].T)
    for s in range(12):
        cols = slice(s * 128, s * 128 + 128)
        r_high, r_low = split(mine[:, cols] + theirs[:, cols])
        core[:, cols] = dot3(y_high, y_low, r_high, r_low, ((1,), (1,)))
    for copy in core_copies(place, core, refs, core_sems):
        copy.start()
    for k in range(12):
        load(k).wait()
        for s in (2 * k, 2 * k + 1):
            rows, cols = slice(s // 12 * 1024, s // 12 * 1024 + 1024), slice(s % 12 * 128, s % 12 * 128 + 128)
            high[rows, cols], low[rows, cols] = split(land[s])
    for b in range(4):
        rows, cols = slice(b * 256, b * 256 + 256), slice(b * 256, b * 256 + 1280)
        buf[b] = dot3(high[rows, :], low[rows, :], high[cols, :], low[cols, :], ((1,), (1,)))
        send_out(place, buf.at[b], b, lambda x: (x // 2) * 128, refs, out_sems)
    wait_out(refs[:6], out_sems)
    for i in range(4):
        part = refs[i].at[:, :, pl.ds(64, 32)]
        pltpu.make_async_copy(part, part, core_sems.at[i]).wait()


def gram_y_kernel(place, own, other, *refs):
    high, low, buf, out_sems = refs[6:]
    for j in range(16):
        tiles = [
            own[j, half : half + 8, s * 128 : s * 128 + 128] + other[j, 8 - half : 16 - half, s * 128 : s * 128 + 128]
            for half in (0, 8)
            for s in range(12)
        ]
        v = jnp.concatenate(tiles + [jnp.zeros((64, 128), F32)], axis=0).T
        v_high, v_low = split(v)
        for start in (j * 128, 2048 + j * 128):
            if start < 3072:
                high[start : start + 128, :] = v_high
                low[start : start + 128, :] = v_low
    h = place[0]
    for b in range(4):
        starts = [pl.multiple_of((b * 4 + x) * 128 + h * 64, 64) for x in range(4)]
        l_high = jnp.concatenate([high[pl.ds(r, 64), :] for r in starts], axis=0)
        l_low = jnp.concatenate([low[pl.ds(r, 64), :] for r in starts], axis=0)
        cols = slice(b * 512, b * 512 + 1536)
        buf[b] = dot3(l_high, l_low, high[cols, :], low[cols, :], ((1,), (1,)))
        send_out(place, buf.at[b], b, lambda x: x * 128, refs, out_sems)
    wait_out(refs[:6], out_sems)


def gram_pieces(kernel, name, rows, place, args, spaces, scratch, flops):
    ab = jax.ShapeDtypeStruct((2, 4, rows, 384), F32)
    c = jax.ShapeDtypeStruct((2, 16, 16, 384), F32)
    return pl.pallas_call(
        kernel,
        in_specs=[pl.BlockSpec(memory_space=space) for space in (pltpu.SMEM,) + spaces],
        out_specs=[pl.BlockSpec(memory_space=pl.ANY)] * 6,
        out_shape=[ab] * 4 + [c] * 2,
        scratch_shapes=scratch,
        compiler_params=pltpu.CompilerParams(vmem_limit_bytes=VMEM_LIMIT),
        cost_estimate=pl.CostEstimate(flops=flops, bytes_accessed=20000000, transcendentals=0),
        name=name,
    )(place, *args)


GRAM_X_SCRATCH = [
    pltpu.VMEM((2048, 1536), BF16),
    pltpu.VMEM((2048, 1536), BF16),
    pltpu.VMEM((4, 256, 1280), F32),
    pltpu.VMEM((24, 1024, 128), F32),
    pltpu.VMEM((256, 1536), F32),
    pltpu.SemaphoreType.DMA((6,)),
    pltpu.SemaphoreType.DMA((12,)),
    pltpu.SemaphoreType.DMA((4,)),
]
GRAM_Y_SCRATCH = [
    pltpu.VMEM((3072, 256), BF16),
    pltpu.VMEM((3072, 256), BF16),
    pltpu.VMEM((4, 256, 1536), F32),
    pltpu.SemaphoreType.DMA((12,)),
]


def sum4(terms, index):
    return (terms[0][index] + terms[1][index]) + (terms[2][index] + terms[3][index])


def add_kernel(*refs):
    for i, out in enumerate(refs[12:]):
        terms = refs[4 * i : 4 * i + 4]
        at = 0
        for kept, came in zip(terms[0::2], terms[1::2]):
            rows = kept.shape[2]
            out[:, at : at + rows, :] = kept[0] + came[0]
            at += rows


def slab_of(v, k):
    return pl.BlockSpec((1,) + v.shape[1:], lambda i: (k, 0, 0, 0))


def add_for_second(*thirds):
    shapes = [(t[0].shape[1], sum(v.shape[2] for v in t[0::2]), 384) for t in thirds]
    terms = [v for t in thirds for v in t]
    return pl.pallas_call(
        add_kernel,
        grid=(1,),
        in_specs=[slab_of(v, 1) for v in terms],
        out_specs=[pl.BlockSpec(shape, lambda i: (0, 0, 0)) for shape in shapes],
        out_shape=[jax.ShapeDtypeStruct(shape, F32) for shape in shapes],
        compiler_params=pltpu.CompilerParams(vmem_limit_bytes=VMEM_LIMIT),
        cost_estimate=pl.CostEstimate(flops=700000, bytes_accessed=9000000, transcendentals=0),
        name="add",
    )(*terms)


def sum_last_third_kernel(k_x, c_x, k_y, c_y, last, out):
    out[:, :16, :] = (k_x[0] + c_x[0]) + last[:, :16, :]
    out[:, 16:, :] = (k_y[0] + c_y[0]) + last[:, 16:, :]


def sum_last_third(terms, last):
    whole = pl.BlockSpec(last.shape, lambda i: (0, 0, 0))
    return pl.pallas_call(
        sum_last_third_kernel,
        grid=(1,),
        in_specs=[slab_of(v, 0) for v in terms] + [whole],
        out_specs=whole,
        out_shape=jax.ShapeDtypeStruct(last.shape, F32),
        compiler_params=pltpu.CompilerParams(vmem_limit_bytes=VMEM_LIMIT),
        cost_estimate=pl.CostEstimate(flops=1000000, bytes_accessed=4000000, transcendentals=0),
        name="sum_last_third",
    )(*terms, last)


def sum_first_kernel(place, *refs):
    for third, axis in enumerate((2, 1)):
        k_x, c_x, k_y, c_y, last = refs[5 * third : 5 * third + 5]
        outs = refs[10 + 2 * third : 12 + 2 * third]
        for sent, slot, mask in owner_masks(place):
            k = place[axis] ^ mask
            outs[sent][slot, :96, :] = (k_x[0, k] + c_x[0, k]) + last[k, :96, :]
            outs[sent][slot, 96:, :] = (k_y[0, k] + c_y[0, k]) + last[k, 96:, :]


def sum_first(place, terms_a, last_a, terms_b, last_b):
    whole = pl.BlockSpec(last_a.shape, lambda i: (0, 0, 0))
    shape = (2, 160, 384)
    return pl.pallas_call(
        sum_first_kernel,
        grid=(1,),
        in_specs=[pl.BlockSpec(memory_space=pltpu.SMEM)]
        + [slab_of(v, 0) for v in terms_a] + [whole]
        + [slab_of(v, 0) for v in terms_b] + [whole],
        out_specs=[pl.BlockSpec(shape, lambda i: (0, 0, 0))] * 4,
        out_shape=[jax.ShapeDtypeStruct(shape, F32)] * 4,
        compiler_params=pltpu.CompilerParams(vmem_limit_bytes=VMEM_LIMIT),
        cost_estimate=pl.CostEstimate(flops=1000000, bytes_accessed=8000000, transcendentals=0),
        name="sum_first",
    )(place, *terms_a, last_a, *terms_b, last_b)


def add_second_kernel(place, k_a, c_a, k_b, c_b, out_a, out_b):
    out_a[...] = k_a[1] + c_a[1]
    out_b[...] = k_b[1] + c_b[1]


def sum_second_kernel(place, *refs):
    outs = refs[6:]
    for part in range(2):
        kept, came, last = refs[part * 3 : part * 3 + 3]

        def total(rows):
            return (kept[0, rows, :] + came[0, rows, :]) + last[rows, :]

        for d in range(4):
            for g in range(2):
                to = part * 32 + g * 16
                rows = pl.ds(pl.multiple_of(g * 96 + ahead(place, 3, d) * 16, 16), 16)
                outs[d][to : to + 16, :] = total(rows)
        outs[4][part * 32 : part * 32 + 32, :] = total(slice(64, 96))


def sum_last_kernel(place, *refs):
    slots, direct_x, keep, give, wide = refs[5:]
    h = place[0]
    j = place[2] * 4 + place[1]
    block_x = h * 8 + j // 2
    parts = [sum4(refs[:4], (slice(0, 32), slice(None))), sum4(refs[:4], (slice(32, 64), slice(None))), refs[4][...]]
    zero = jnp.zeros((16, 128), F32)
    for k in range(16):
        lane = k % 3 * 128
        tile_x = parts[k // 3][:16, lane : lane + 128] if k < 9 else zero
        tile_y = parts[k // 3][16:, lane : lane + 128] if k < 9 else zero
        to_x, to_y = lax.rem(block_x + k, 16), lax.rem(j + k, 16)
        direct_x[to_x] = tile_x
        wide[lax.rem(to_y + 8 * h, 16)] = tile_y
        for e in range(2):
            half = tile_x[:, e * 64 : e * 64 + 64]
            slots[2 * to_x + e, 16:] = jnp.concatenate([half[:8], half[8:]], axis=1)
            slots[16 * e + to_y, :16] = tile_y
    keep[...] = wide[:8]
    give[...] = wide[8:]


def select_kernel(place, got, direct_x, keep, come, out):
    h = place[0]
    j = place[2] * 4 + place[1]
    block_x = h * 8 + j // 2
    for block in range(16):
        first, second = got[2 * block, 16:], got[2 * block + 1, 16:]
        turned = jnp.concatenate(
            [jnp.concatenate([t[:, :64] for t in (first, second)], axis=1), jnp.concatenate([t[:, 64:] for t in (first, second)], axis=1)],
            axis=0,
        )
        out[block] = jnp.where(lax.rem(block - block_x + 16, 16) <= 8, direct_x[block], turned)
    for block in range(8):
        is_direct = lax.rem(h * 8 + block - j + 16, 16) <= 8
        for half in range(2):
            direct = jnp.where(h == half, keep[block], come[block])
            out[16 + 2 * block + half] = jnp.where(is_direct, direct, got[half * 16 + h * 8 + block, :16])


def assemble_kernel(scale_x, scale_y, place, q0, q1, q2, q3, gram_x, gram_y, rows):
    h = place[0]
    j = place[2] * 4 + place[1]
    block_x = h * 8 + j // 2
    for quarter, mask in zip((q0, q1, q2, q3), (0, place[4], 4 - place[4], 2)):
        z = place[3] ^ mask
        rows[:, pl.ds(pl.multiple_of(z * 16, 16), 16), :] = quarter[...]
    for block in range(16):
        direct = rows[block]
        turned = direct.T
        turned = jnp.concatenate([turned[:64], turned[64:]], axis=1)
        is_direct = lax.rem(block - block_x + 16, 16) <= 8
        gram_x[:, block * 128 : block * 128 + 128] = jnp.where(is_direct, direct, turned) * scale_x
    for block in range(8):
        direct = jnp.concatenate([rows[16 + 2 * block], rows[17 + 2 * block]], axis=0)
        is_direct = lax.rem(h * 8 + block - j + 16, 16) <= 8
        gram_y[:, block * 128 : block * 128 + 128] = jnp.where(is_direct, direct, direct.T) * scale_y


def small_kernel(kernel, name, out_shape, scratch, *args):
    return pl.pallas_call(
        kernel,
        in_specs=[pl.BlockSpec(memory_space=pltpu.SMEM)] + [pl.BlockSpec(memory_space=pltpu.VMEM)] * (len(args) - 1),
        out_shape=out_shape,
        scratch_shapes=scratch,
        compiler_params=pltpu.CompilerParams(vmem_limit_bytes=VMEM_LIMIT),
        name=name,
    )(*args)


def per_device(species_field, x_mode_basis, y_mode_basis):
    h, j, z0 = lax.axis_index("gx"), lax.axis_index("gy"), lax.axis_index("gz")
    x0, y0 = j % 4, j // 4
    place = jnp.stack([h, x0, y0, z0, 1 + 2 * h]).astype(jnp.int32)
    nx = 2 * species_field.shape[1]
    ny = 16 * species_field.shape[2]
    slices = 4 * species_field.shape[0]
    ranks = x_mode_basis.shape[1]

    other_field = lax.ppermute(species_field, "gx", SWAP)
    mine, give, both = project(place, species_field, x_mode_basis)
    theirs = lax.ppermute(give, "gx", SWAP)
    fibers = lax.all_to_all(both, "gy", 0, 0, tiled=True)

    def first_swaps(pieces):
        return [swap(pieces[2 * i + 1], 0) for i, swap in enumerate((swap_x, swap_y, swap_z))]

    px = gram_pieces(
        gram_x_kernel, "gram_x", 96, place, (species_field, other_field, mine, theirs, y_mode_basis),
        (pl.ANY, pl.ANY, pltpu.VMEM, pltpu.VMEM, pltpu.VMEM), GRAM_X_SCRATCH, 12000000000,
    )
    px, fibers = lax.optimization_barrier((px, fibers))
    other_fibers = lax.ppermute(fibers, "gx", SWAP)
    came_x = first_swaps(px)
    py = gram_pieces(
        gram_y_kernel, "gram_y", 64, place, (fibers, other_fibers), (pltpu.VMEM, pltpu.VMEM), GRAM_Y_SCRATCH, 2400000000
    )
    came_y = first_swaps(py)

    terms_a, terms_b, terms_c = [(px[2 * i], came_x[i], py[2 * i], came_y[i]) for i in range(3)]
    last_a, last_b, last_c = add_for_second(terms_a, terms_b, terms_c)
    kept_a, sent_a, kept_b, sent_b = sum_first(place, terms_a, swap_x(last_a, 1), terms_b, swap_y(last_b, 1))
    came_a, came_b = swap_y(sent_a, 0), swap_x(sent_b, 0)
    last_c, kept_a = lax.optimization_barrier((swap_z(last_c, 1), kept_a))
    c = lax.all_to_all(sum_last_third(terms_c, last_c), "gy", 0, 0, tiled=True).sum(axis=0)
    second = jax.ShapeDtypeStruct((160, 384), F32)
    last_a, last_b = small_kernel(
        add_second_kernel, "add_second", [second] * 2, [], place, kept_a, came_a, kept_b, came_b
    )
    part = jax.ShapeDtypeStruct((64, 384), F32)
    *quarters, core = small_kernel(
        sum_second_kernel, "sum_second", [part] * 5, [],
        place, kept_a, came_a, swap_y(last_a, 1), kept_b, came_b, swap_x(last_b, 1),
    )
    blocks = jax.ShapeDtypeStruct((8, 16, 128), F32)
    slots, direct_x, keep, give = small_kernel(
        sum_last_kernel, "sum_last",
        [jax.ShapeDtypeStruct((32, 24, 128), F32), jax.ShapeDtypeStruct((16, 16, 128), F32), blocks, blocks],
        [pltpu.VMEM((16, 16, 128), F32)],
        place, *[quarters[0]] + [shift_z(quarters[d], d) for d in (1, 2, 3)], c,
    )
    core = core.reshape(2, 2, 16, 3, 128).transpose(4, 0, 1, 3, 2).reshape(128, 12, 16)

    got = lax.all_to_all(slots, ("gx", "gy"), 0, 0, tiled=True)
    come = lax.ppermute(give, "gx", SWAP)
    part = small_kernel(
        select_kernel, "select", jax.ShapeDtypeStruct((32, 16, 128), F32), [], place, got, direct_x, keep, come
    )
    first = swap_z(part, 0)
    quarters = [part, first, swap_z(part, 1), swap_z(first, 1)]
    gram_x, gram_y = small_kernel(
        functools.partial(assemble_kernel, 1.0 / (ny * slices), 1.0 / (ranks * slices)),
        "assemble",
        [jax.ShapeDtypeStruct((64, nx), F32), jax.ShapeDtypeStruct((128, ny // 2), F32)],
        [pltpu.VMEM((32, 64, 128), F32)],
        place, *quarters,
    )
    return (gram_x, gram_y, core)


def solution(mesh):
    in_specs = (P("gz", "gx", "gy"), P("gx", None), P("gy", None))
    out_specs = (P(("gx", "gy"), None), P("gy", "gx"), P("gx", "gz", "gy"))
    return jax.shard_map(
        per_device, mesh=mesh, in_specs=in_specs, out_specs=out_specs, check_vma=False
    )
```

```python
import functools

import jax
import jax.numpy as jnp
from jax import lax
from jax.experimental import pallas as pl
from jax.experimental.pallas import tpu as pltpu
from jax.sharding import PartitionSpec as P

F32 = jnp.float32
BF16 = jnp.bfloat16
VMEM_LIMIT = 58 * 1024 * 1024

SWAP = [(0, 1), (1, 0)]


def device(h, y, x, z):
    return (h * 16 + y % 4 * 4 + x % 4) * 4 + z % 4


def stepper(axis):
    def step(v, d):
        pairs = []
        for h in range(2):
            by = d if h == 0 else -d
            move = [by if name == axis else 0 for name in "yxz"]
            for y in range(4):
                for x in range(4):
                    for z in range(4):
                        pairs.append((device(h, y, x, z), device(h, y + move[0], x + move[1], z + move[2])))
        return lax.ppermute(v, ("gx", "gy", "gz"), pairs)

    return step


shift_x, shift_y, shift_z = stepper("x"), stepper("y"), stepper("z")


def swapper(axis):
    def swap(v, turn):
        pairs = []
        for h in range(2):
            mask = 1 if h == turn else 3
            for y in range(4):
                for x in range(4):
                    for z in range(4):
                        to = [c ^ mask if name == axis else c for name, c in zip("yxz", (y, x, z))]
                        pairs.append((device(h, y, x, z), device(h, *to)))
        return lax.ppermute(v, ("gx", "gy", "gz"), pairs)

    return swap


swap_x, swap_y, swap_z = swapper("x"), swapper("y"), swapper("z")


def ahead(place, axis, d):
    return lax.rem(place[axis] + d * place[4], 4)


def owner_masks(place):
    return ((0, 0, 0), (1, 0, place[4]), (1, 1, 2), (0, 1, 4 - place[4]))


def split(v):
    high = v.astype(BF16)
    return high, (v - high.astype(F32)).astype(BF16)


def dot3(a_high, a_low, b_high, b_low, dims):
    dot = functools.partial(lax.dot_general, dimension_numbers=(dims, ((), ())), preferred_element_type=F32)
    return dot(a_high, b_high) + (dot(a_high, b_low) + dot(a_low, b_high))


def project_kernel(place, field, basis, own, other, both, land, x_land, x_high, x_low, f_high, f_low, sems):
    def load(k):
        part = pl.ds(k * 2, 2)
        return pltpu.make_async_copy(field.at[part], land.at[part], sems.at[k])

    x_load = pltpu.make_async_copy(basis, x_land, sems.at[6])
    x_load.start()
    for k in range(6):
        load(k).start()
    x_load.wait()
    turned = x_land[...].T
    for half in range(2):
        rows = pl.ds(pl.multiple_of((place[0] ^ half) * 128, 128), 128)
        x_high[rows, :], x_low[rows, :] = split(turned[half * 128 : half * 128 + 128])
    for k in range(6):
        load(k).wait()
        for s in (2 * k, 2 * k + 1):
            f_high[:, s * 128 : s * 128 + 128], f_low[:, s * 128 : s * 128 + 128] = split(land[s])
    out = dot3(x_high[...], x_low[...], f_high[...], f_low[...], ((1,), (0,)))
    own[...] = out[:128]
    other[...] = out[128:]
    for j in range(16):
        both[j, :8] = out[j * 8 : j * 8 + 8]
        both[j, 8:] = out[128 + j * 8 : 136 + j * 8]


def project(place, field, basis):
    out = jax.ShapeDtypeStruct((128, 1536), F32)
    return pl.pallas_call(
        project_kernel,
        in_specs=[pl.BlockSpec(memory_space=pltpu.SMEM)] + [pl.BlockSpec(memory_space=pl.ANY)] * 2,
        out_specs=[pl.BlockSpec(memory_space=pltpu.VMEM)] * 3,
        out_shape=[out, out, jax.ShapeDtypeStruct((16, 16, 1536), F32)],
        scratch_shapes=[
            pltpu.VMEM((12, 1024, 128), F32),
            pltpu.VMEM((1024, 256), F32),
            pltpu.VMEM((256, 1024), BF16),
            pltpu.VMEM((256, 1024), BF16),
            pltpu.VMEM((1024, 1536), BF16),
            pltpu.VMEM((1024, 1536), BF16),
            pltpu.SemaphoreType.DMA((7,)),
        ],
        compiler_params=pltpu.CompilerParams(vmem_limit_bytes=VMEM_LIMIT),
        cost_estimate=pl.CostEstimate(flops=2400000000, bytes_accessed=9000000, transcendentals=0),
        name="project",
    )(place, field, basis)


def send_out(place, buf, b, lane_of, refs, sems):
    def piece(x, row, rows, third):
        row = pl.multiple_of(x * 64 + row, 16)
        return buf.at[pl.ds(row, rows), pl.ds(pl.multiple_of(lane_of(x) + third * 384, 128), 384)]

    rows = pl.ds(0, 64)
    for sent, slot, mask in owner_masks(place):
        x, z = place[1] ^ mask, place[3] ^ mask
        pltpu.make_async_copy(piece(x, 0, 64, 0), refs[sent].at[slot, b, rows], sems.at[sent]).start()

        @pl.when(place[2] ^ mask == b)
        def _():
            for x in range(4):
                pltpu.make_async_copy(piece(x, 0, 64, 1), refs[2 + sent].at[slot, x, rows], sems.at[2 + sent]).start()

        for x in range(4):
            to = refs[4 + sent].at[slot, b * 4 + x]
            pltpu.make_async_copy(piece(x, z * 16, 16, 2), to, sems.at[4 + sent]).start()


def wait_out(refs, sems):
    for i, ref in enumerate(refs):
        part = ref.at[:, :, pl.ds(0, 64)] if i < 4 else ref
        pltpu.make_async_copy(part, part, sems.at[i]).wait()


def core_copies(place, buf, refs, sems):
    copies = []
    for sent, slot, mask in owner_masks(place):
        for other in range(4):
            for half in range(2):
                rows = pl.ds(64 + half * 16, 16)
                q = pl.multiple_of((other * 4 + (place[1] ^ mask)) * 16, 16)
                src = buf.at[pl.ds(q, 16), pl.ds(half * 384, 384)]
                copies.append(pltpu.make_async_copy(src, refs[sent].at[slot, other, rows], sems.at[sent]))
                q = pl.multiple_of(((place[2] ^ mask) * 4 + other) * 16, 16)
                src = buf.at[pl.ds(q, 16), pl.ds(768 + half * 384, 384)]
                copies.append(pltpu.make_async_copy(src, refs[2 + sent].at[slot, other, rows], sems.at[2 + sent]))
    return copies


def gram_x_kernel(place, own, other, mine, theirs, y_basis, *refs):
    high, low, buf, land, core, out_sems, sems, core_sems = refs[6:]

    def load(k):
        src = own if k < 6 else other
        part = pl.ds(k % 6 * 2, 2)
        return pltpu.make_async_copy(src.at[part], land.at[pl.ds(k * 2, 2)], sems.at[k])

    for k in range(12):
        load(k).start()
    y_high, y_low = split(y_basis[...].T)
    for s in range(12):
        cols = slice(s * 128, s * 128 + 128)
        r_high, r_low = split(mine[:, cols] + theirs[:, cols])
        core[:, cols] = dot3(y_high, y_low, r_high, r_low, ((1,), (1,)))
    for copy in core_copies(place, core, refs, core_sems):
        copy.start()
    for k in range(12):
        load(k).wait()
        for s in (2 * k, 2 * k + 1):
            rows, cols = slice(s // 12 * 1024, s // 12 * 1024 + 1024), slice(s % 12 * 128, s % 12 * 128 + 128)
            high[rows, cols], low[rows, cols] = split(land[s])
    for b in range(4):
        rows, cols = slice(b * 256, b * 256 + 256), slice(b * 256, b * 256 + 1280)
        buf[b] = dot3(high[rows, :], low[rows, :], high[cols, :], low[cols, :], ((1,), (1,)))
        send_out(place, buf.at[b], b, lambda x: (x // 2) * 128, refs, out_sems)
    wait_out(refs[:6], out_sems)
    for i in range(4):
        part = refs[i].at[:, :, pl.ds(64, 32)]
        pltpu.make_async_copy(part, part, core_sems.at[i]).wait()


def gram_y_kernel(place, own, other, *refs):
    high, low, buf, out_sems = refs[6:]
    for j in range(16):
        tiles = [
            own[j, half : half + 8, s * 128 : s * 128 + 128] + other[j, 8 - half : 16 - half, s * 128 : s * 128 + 128]
            for half in (0, 8)
            for s in range(12)
        ]
        v = jnp.concatenate(tiles + [jnp.zeros((64, 128), F32)], axis=0).T
        v_high, v_low = split(v)
        for start in (j * 128, 2048 + j * 128):
            if start < 3072:
                high[start : start + 128, :] = v_high
                low[start : start + 128, :] = v_low
    h = place[0]
    for b in range(4):
        starts = [pl.multiple_of((b * 4 + x) * 128 + h * 64, 64) for x in range(4)]
        l_high = jnp.concatenate([high[pl.ds(r, 64), :] for r in starts], axis=0)
        l_low = jnp.concatenate([low[pl.ds(r, 64), :] for r in starts], axis=0)
        cols = slice(b * 512, b * 512 + 1536)
        buf[b] = dot3(l_high, l_low, high[cols, :], low[cols, :], ((1,), (1,)))
        send_out(place, buf.at[b], b, lambda x: x * 128, refs, out_sems)
    wait_out(refs[:6], out_sems)


def gram_pieces(kernel, name, rows, place, args, spaces, scratch, flops):
    ab = jax.ShapeDtypeStruct((2, 4, rows, 384), F32)
    c = jax.ShapeDtypeStruct((2, 16, 16, 384), F32)
    return pl.pallas_call(
        kernel,
        in_specs=[pl.BlockSpec(memory_space=space) for space in (pltpu.SMEM,) + spaces],
        out_specs=[pl.BlockSpec(memory_space=pl.ANY)] * 6,
        out_shape=[ab] * 4 + [c] * 2,
        scratch_shapes=scratch,
        compiler_params=pltpu.CompilerParams(vmem_limit_bytes=VMEM_LIMIT),
        cost_estimate=pl.CostEstimate(flops=flops, bytes_accessed=20000000, transcendentals=0),
        name=name,
    )(place, *args)


GRAM_X_SCRATCH = [
    pltpu.VMEM((2048, 1536), BF16),
    pltpu.VMEM((2048, 1536), BF16),
    pltpu.VMEM((4, 256, 1280), F32),
    pltpu.VMEM((24, 1024, 128), F32),
    pltpu.VMEM((256, 1536), F32),
    pltpu.SemaphoreType.DMA((6,)),
    pltpu.SemaphoreType.DMA((12,)),
    pltpu.SemaphoreType.DMA((4,)),
]
GRAM_Y_SCRATCH = [
    pltpu.VMEM((3072, 256), BF16),
    pltpu.VMEM((3072, 256), BF16),
    pltpu.VMEM((4, 256, 1536), F32),
    pltpu.SemaphoreType.DMA((12,)),
]


def sum4(terms, index):
    return (terms[0][index] + terms[1][index]) + (terms[2][index] + terms[3][index])


def slab_of(v, k):
    return pl.BlockSpec((1,) + v.shape[1:], lambda i: (k, 0, 0, 0))


def shapes_of(px, py):
    return [jax.ShapeDtypeStruct((v.shape[1], v.shape[2] + w.shape[2], 384), F32) for v, w in zip(px, py)]


def add_x_kernel(*refs):
    for kept, came, out in zip(refs[0:3], refs[3:6], refs[6:9]):
        out[...] = kept[0] + came[0]


def add_x(kept, came, shapes):
    return pl.pallas_call(
        add_x_kernel,
        grid=(1,),
        in_specs=[slab_of(v, 1) for v in kept + came],
        out_specs=[pl.BlockSpec(v.shape[1:], lambda i: (0, 0, 0)) for v in kept],
        out_shape=shapes,
        compiler_params=pltpu.CompilerParams(vmem_limit_bytes=VMEM_LIMIT),
        cost_estimate=pl.CostEstimate(flops=400000, bytes_accessed=5000000, transcendentals=0),
        name="add_x",
    )(*kept, *came)


def add_y_kernel(*refs):
    for kept, came, out in zip(refs[0:3], refs[3:6], refs[9:12]):
        out[...] = kept[0] + came[0]


def add_y(kept, came, sums):
    ins, outs = [], []
    for v, total in zip(kept, sums):
        rows = v.shape[2] // 2
        first = total.shape[1] // rows - 2
        ins.append(pl.BlockSpec((1, v.shape[1], rows, 384), lambda i: (1, 0, i, 0)))
        outs.append(pl.BlockSpec((v.shape[1], rows, 384), lambda i, first=first: (0, first + i, 0)))
    return pl.pallas_call(
        add_y_kernel,
        grid=(2,),
        in_specs=ins + ins + [pl.BlockSpec(memory_space=pl.ANY)] * 3,
        out_specs=outs,
        out_shape=[jax.ShapeDtypeStruct(v.shape, F32) for v in sums],
        input_output_aliases={6: 0, 7: 1, 8: 2},
        compiler_params=pltpu.CompilerParams(vmem_limit_bytes=VMEM_LIMIT),
        cost_estimate=pl.CostEstimate(flops=300000, bytes_accessed=4000000, transcendentals=0),
        name="add_y",
    )(*kept, *came, *sums)


def add_own_kernel(*refs):
    for k_x, c_x, k_y, c_y, out in zip(refs[0:3], refs[3:6], refs[6:9], refs[9:12], refs[12:15]):
        rows = k_x.shape[2]
        out[:, :rows, :] = k_x[0] + c_x[0]
        out[:, rows:, :] = k_y[0] + c_y[0]


def add_own(terms, shapes):
    return pl.pallas_call(
        add_own_kernel,
        grid=(1,),
        in_specs=[slab_of(v, 0) for v in terms],
        out_specs=[pl.BlockSpec(v.shape, lambda i: (0, 0, 0)) for v in shapes],
        out_shape=shapes,
        compiler_params=pltpu.CompilerParams(vmem_limit_bytes=VMEM_LIMIT),
        cost_estimate=pl.CostEstimate(flops=700000, bytes_accessed=9000000, transcendentals=0),
        name="add_own",
    )(*terms)


def sum_first_kernel(place, own_a, last_a, own_b, last_b, *outs):
    for axis, own, last, out in ((2, own_a, last_a, outs[0:2]), (1, own_b, last_b, outs[2:4])):
        for sent, slot, mask in owner_masks(place):
            k = place[axis] ^ mask
            out[sent][slot] = own[k] + last[k]


def add_two_kernel(place, first, second, out):
    out[...] = first[...] + second[...]


def add_second_kernel(place, k_a, c_a, k_b, c_b, out_a, out_b):
    out_a[...] = k_a[1] + c_a[1]
    out_b[...] = k_b[1] + c_b[1]


def sum_second_kernel(place, *refs):
    outs = refs[6:]
    for part in range(2):
        kept, came, last = refs[part * 3 : part * 3 + 3]

        def total(rows):
            return (kept[0, rows, :] + came[0, rows, :]) + last[rows, :]

        for d in range(4):
            for g in range(2):
                to = part * 32 + g * 16
                rows = pl.ds(pl.multiple_of(g * 96 + ahead(place, 3, d) * 16, 16), 16)
                outs[d][to : to + 16, :] = total(rows)
        outs[4][part * 32 : part * 32 + 32, :] = total(slice(64, 96))


def sum_last_kernel(place, *refs):
    slots, direct_x, keep, give, wide = refs[5:]
    h = place[0]
    j = place[2] * 4 + place[1]
    block_x = h * 8 + j // 2
    parts = [sum4(refs[:4], (slice(0, 32), slice(None))), sum4(refs[:4], (slice(32, 64), slice(None))), refs[4][...]]
    zero = jnp.zeros((16, 128), F32)
    for k in range(16):
        lane = k % 3 * 128
        tile_x = parts[k // 3][:16, lane : lane + 128] if k < 9 else zero
        tile_y = parts[k // 3][16:, lane : lane + 128] if k < 9 else zero
        to_x, to_y = lax.rem(block_x + k, 16), lax.rem(j + k, 16)
        direct_x[to_x] = tile_x
        wide[lax.rem(to_y + 8 * h, 16)] = tile_y
        for e in range(2):
            half = tile_x[:, e * 64 : e * 64 + 64]
            slots[2 * to_x + e, 16:] = jnp.concatenate([half[:8], half[8:]], axis=1)
            slots[16 * e + to_y, :16] = tile_y
    keep[...] = wide[:8]
    give[...] = wide[8:]


def select_kernel(place, got, direct_x, keep, come, out):
    h = place[0]
    j = place[2] * 4 + place[1]
    block_x = h * 8 + j // 2
    for block in range(16):
        first, second = got[2 * block, 16:], got[2 * block + 1, 16:]
        turned = jnp.concatenate(
            [jnp.concatenate([t[:, :64] for t in (first, second)], axis=1), jnp.concatenate([t[:, 64:] for t in (first, second)], axis=1)],
            axis=0,
        )
        out[block] = jnp.where(lax.rem(block - block_x + 16, 16) <= 8, direct_x[block], turned)
    for block in range(8):
        is_direct = lax.rem(h * 8 + block - j + 16, 16) <= 8
        for half in range(2):
            direct = jnp.where(h == half, keep[block], come[block])
            out[16 + 2 * block + half] = jnp.where(is_direct, direct, got[half * 16 + h * 8 + block, :16])


def assemble_kernel(scale_x, scale_y, place, q0, q1, q2, q3, gram_x, gram_y, rows):
    h = place[0]
    j = place[2] * 4 + place[1]
    block_x = h * 8 + j // 2
    for quarter, mask in zip((q0, q1, q2, q3), (0, place[4], 4 - place[4], 2)):
        z = place[3] ^ mask
        rows[:, pl.ds(pl.multiple_of(z * 16, 16), 16), :] = quarter[...]
    for block in range(16):
        direct = rows[block]
        turned = direct.T
        turned = jnp.concatenate([turned[:64], turned[64:]], axis=1)
        is_direct = lax.rem(block - block_x + 16, 16) <= 8
        gram_x[:, block * 128 : block * 128 + 128] = jnp.where(is_direct, direct, turned) * scale_x
    for block in range(8):
        direct = jnp.concatenate([rows[16 + 2 * block], rows[17 + 2 * block]], axis=0)
        is_direct = lax.rem(h * 8 + block - j + 16, 16) <= 8
        gram_y[:, block * 128 : block * 128 + 128] = jnp.where(is_direct, direct, direct.T) * scale_y


def small_kernel(kernel, name, out_shape, scratch, *args):
    return pl.pallas_call(
        kernel,
        in_specs=[pl.BlockSpec(memory_space=pltpu.SMEM)] + [pl.BlockSpec(memory_space=pltpu.VMEM)] * (len(args) - 1),
        out_shape=out_shape,
        scratch_shapes=scratch,
        compiler_params=pltpu.CompilerParams(vmem_limit_bytes=VMEM_LIMIT),
        name=name,
    )(*args)


def per_device(species_field, x_mode_basis, y_mode_basis):
    h, j, z0 = lax.axis_index("gx"), lax.axis_index("gy"), lax.axis_index("gz")
    x0, y0 = j % 4, j // 4
    place = jnp.stack([h, x0, y0, z0, 1 + 2 * h]).astype(jnp.int32)
    nx = 2 * species_field.shape[1]
    ny = 16 * species_field.shape[2]
    slices = 4 * species_field.shape[0]
    ranks = x_mode_basis.shape[1]

    other_field = lax.ppermute(species_field, "gx", SWAP)
    mine, give, both = project(place, species_field, x_mode_basis)
    theirs = lax.ppermute(give, "gx", SWAP)
    fibers = lax.all_to_all(both, "gy", 0, 0, tiled=True)

    def first_swaps(pieces):
        return [swap(pieces[2 * i + 1], 0) for i, swap in enumerate((swap_x, swap_y, swap_z))]

    px = gram_pieces(
        gram_x_kernel, "gram_x", 96, place, (species_field, other_field, mine, theirs, y_mode_basis),
        (pl.ANY, pl.ANY, pltpu.VMEM, pltpu.VMEM, pltpu.VMEM), GRAM_X_SCRATCH, 12000000000,
    )
    px, fibers = lax.optimization_barrier((px, fibers))
    other_fibers = lax.ppermute(fibers, "gx", SWAP)
    came_x = first_swaps(px)
    py = gram_pieces(
        gram_y_kernel, "gram_y", 64, place, (fibers, other_fibers), (pltpu.VMEM, pltpu.VMEM), GRAM_Y_SCRATCH, 2400000000
    )
    came_y = first_swaps(py)

    kept_x, kept_y = list(px[0::2]), list(py[0::2])
    shapes = shapes_of(kept_x, kept_y)
    last = add_y(kept_y, came_y, add_x(kept_x, came_x, shapes))
    *terms, last = lax.optimization_barrier((*kept_x, *came_x, *kept_y, *came_y, last))
    own_a, own_b, own_c = add_own(terms, shapes)
    last_a, last_b, last_c = [swap(v, 1) for v, swap in zip(last, (swap_x, swap_y, swap_z))]
    halves = jax.ShapeDtypeStruct((2, 160, 384), F32)
    kept_a, sent_a, kept_b, sent_b = small_kernel(
        sum_first_kernel, "sum_first", [halves] * 4, [], place, own_a, last_a, own_b, last_b
    )
    came_a, came_b = swap_y(sent_a, 0), swap_x(sent_b, 0)
    last_c, kept_a = lax.optimization_barrier((last_c, kept_a))
    c = small_kernel(add_two_kernel, "sum_last_third", shapes[2], [], place, own_c, last_c)
    c = lax.all_to_all(c, "gy", 0, 0, tiled=True).sum(axis=0)
    second = jax.ShapeDtypeStruct((160, 384), F32)
    last_a, last_b = small_kernel(
        add_second_kernel, "add_second", [second] * 2, [], place, kept_a, came_a, kept_b, came_b
    )
    part = jax.ShapeDtypeStruct((64, 384), F32)
    *quarters, core = small_kernel(
        sum_second_kernel, "sum_second", [part] * 5, [],
        place, kept_a, came_a, swap_y(last_a, 1), kept_b, came_b, swap_x(last_b, 1),
    )
    blocks = jax.ShapeDtypeStruct((8, 16, 128), F32)
    slots, direct_x, keep, give = small_kernel(
        sum_last_kernel, "sum_last",
        [jax.ShapeDtypeStruct((32, 24, 128), F32), jax.ShapeDtypeStruct((16, 16, 128), F32), blocks, blocks],
        [pltpu.VMEM((16, 16, 128), F32)],
        place, *[quarters[0]] + [shift_z(quarters[d], d) for d in (1, 2, 3)], c,
    )
    core = core.reshape(2, 2, 16, 3, 128).transpose(4, 0, 1, 3, 2).reshape(128, 12, 16)

    got = lax.all_to_all(slots, ("gx", "gy"), 0, 0, tiled=True)
    come = lax.ppermute(give, "gx", SWAP)
    part = small_kernel(
        select_kernel, "select", jax.ShapeDtypeStruct((32, 16, 128), F32), [], place, got, direct_x, keep, come
    )
    first = swap_z(part, 0)
    quarters = [part, first, swap_z(part, 1), swap_z(first, 1)]
    gram_x, gram_y = small_kernel(
        functools.partial(assemble_kernel, 1.0 / (ny * slices), 1.0 / (ranks * slices)),
        "assemble",
        [jax.ShapeDtypeStruct((64, nx), F32), jax.ShapeDtypeStruct((128, ny // 2), F32)],
        [pltpu.VMEM((32, 64, 128), F32)],
        place, *quarters,
    )
    return (gram_x, gram_y, core)


def solution(mesh):
    in_specs = (P("gz", "gx", "gy"), P("gx", None), P("gy", None))
    out_specs = (P(("gx", "gy"), None), P("gy", "gx"), P("gx", "gz", "gy"))
    return jax.shard_map(
        per_device, mesh=mesh, in_specs=in_specs, out_specs=out_specs, check_vma=False
    )
```

```python
import functools

import jax
import jax.numpy as jnp
from jax import lax
from jax.experimental import pallas as pl
from jax.experimental.pallas import tpu as pltpu
from jax.sharding import PartitionSpec as P

F32 = jnp.float32
BF16 = jnp.bfloat16
VMEM_LIMIT = 58 * 1024 * 1024

SWAP = [(0, 1), (1, 0)]


def device(h, y, x, z):
    return (h * 16 + y % 4 * 4 + x % 4) * 4 + z % 4


def stepper(axis):
    def step(v, d):
        pairs = []
        for h in range(2):
            by = d if h == 0 else -d
            move = [by if name == axis else 0 for name in "yxz"]
            for y in range(4):
                for x in range(4):
                    for z in range(4):
                        pairs.append((device(h, y, x, z), device(h, y + move[0], x + move[1], z + move[2])))
        return lax.ppermute(v, ("gx", "gy", "gz"), pairs)

    return step


shift_x, shift_y, shift_z = stepper("x"), stepper("y"), stepper("z")


def swapper(axis):
    def swap(v, turn):
        pairs = []
        for h in range(2):
            mask = 1 if h == turn else 3
            for y in range(4):
                for x in range(4):
                    for z in range(4):
                        to = [c ^ mask if name == axis else c for name, c in zip("yxz", (y, x, z))]
                        pairs.append((device(h, y, x, z), device(h, *to)))
        return lax.ppermute(v, ("gx", "gy", "gz"), pairs)

    return swap


swap_x, swap_y, swap_z = swapper("x"), swapper("y"), swapper("z")


def ahead(place, axis, d):
    return lax.rem(place[axis] + d * place[4], 4)


def owner_masks(place):
    return ((0, 0, 0), (1, 0, place[4]), (1, 1, 2), (0, 1, 4 - place[4]))


def split(v):
    high = v.astype(BF16)
    return high, (v - high.astype(F32)).astype(BF16)


def dot3(a_high, a_low, b_high, b_low, dims):
    dot = functools.partial(lax.dot_general, dimension_numbers=(dims, ((), ())), preferred_element_type=F32)
    return dot(a_high, b_high) + (dot(a_high, b_low) + dot(a_low, b_high))


def project_kernel(place, field, basis, own, other, both, land, x_land, x_high, x_low, f_high, f_low, sems):
    def load(k):
        part = pl.ds(k * 2, 2)
        return pltpu.make_async_copy(field.at[part], land.at[part], sems.at[k])

    x_load = pltpu.make_async_copy(basis, x_land, sems.at[6])
    x_load.start()
    for k in range(6):
        load(k).start()
    x_load.wait()
    turned = x_land[...].T
    for half in range(2):
        rows = pl.ds(pl.multiple_of((place[0] ^ half) * 128, 128), 128)
        x_high[rows, :], x_low[rows, :] = split(turned[half * 128 : half * 128 + 128])
    for k in range(6):
        load(k).wait()
        for s in (2 * k, 2 * k + 1):
            f_high[:, s * 128 : s * 128 + 128], f_low[:, s * 128 : s * 128 + 128] = split(land[s])
    out = dot3(x_high[...], x_low[...], f_high[...], f_low[...], ((1,), (0,)))
    own[...] = out[:128]
    other[...] = out[128:]
    for j in range(16):
        both[j, :8] = out[j * 8 : j * 8 + 8]
        both[j, 8:] = out[128 + j * 8 : 136 + j * 8]


def project(place, field, basis):
    out = jax.ShapeDtypeStruct((128, 1536), F32)
    return pl.pallas_call(
        project_kernel,
        in_specs=[pl.BlockSpec(memory_space=pltpu.SMEM)] + [pl.BlockSpec(memory_space=pl.ANY)] * 2,
        out_specs=[pl.BlockSpec(memory_space=pltpu.VMEM)] * 3,
        out_shape=[out, out, jax.ShapeDtypeStruct((16, 16, 1536), F32)],
        scratch_shapes=[
            pltpu.VMEM((12, 1024, 128), F32),
            pltpu.VMEM((1024, 256), F32),
            pltpu.VMEM((256, 1024), BF16),
            pltpu.VMEM((256, 1024), BF16),
            pltpu.VMEM((1024, 1536), BF16),
            pltpu.VMEM((1024, 1536), BF16),
            pltpu.SemaphoreType.DMA((7,)),
        ],
        compiler_params=pltpu.CompilerParams(vmem_limit_bytes=VMEM_LIMIT),
        cost_estimate=pl.CostEstimate(flops=2400000000, bytes_accessed=9000000, transcendentals=0),
        name="project",
    )(place, field, basis)


def send_out(place, buf, b, lane_of, refs, sems):
    def piece(x, row, rows, third):
        row = pl.multiple_of(x * 64 + row, 16)
        return buf.at[pl.ds(row, rows), pl.ds(pl.multiple_of(lane_of(x) + third * 384, 128), 384)]

    rows = pl.ds(0, 64)
    for sent, slot, mask in owner_masks(place):
        x, z = place[1] ^ mask, place[3] ^ mask
        pltpu.make_async_copy(piece(x, 0, 64, 0), refs[sent].at[slot, b, rows], sems.at[sent]).start()

        @pl.when(place[2] ^ mask == b)
        def _():
            for x in range(4):
                pltpu.make_async_copy(piece(x, 0, 64, 1), refs[2 + sent].at[slot, x, rows], sems.at[2 + sent]).start()

        for x in range(4):
            to = refs[4 + sent].at[slot, b * 4 + x]
            pltpu.make_async_copy(piece(x, z * 16, 16, 2), to, sems.at[4 + sent]).start()


def wait_out(refs, sems):
    for i, ref in enumerate(refs):
        part = ref.at[:, :, pl.ds(0, 64)] if i < 4 else ref
        pltpu.make_async_copy(part, part, sems.at[i]).wait()


def core_copies(place, buf, refs, sems):
    copies = []
    for sent, slot, mask in owner_masks(place):
        for other in range(4):
            for half in range(2):
                rows = pl.ds(64 + half * 16, 16)
                q = pl.multiple_of((other * 4 + (place[1] ^ mask)) * 16, 16)
                src = buf.at[pl.ds(q, 16), pl.ds(half * 384, 384)]
                copies.append(pltpu.make_async_copy(src, refs[sent].at[slot, other, rows], sems.at[sent]))
                q = pl.multiple_of(((place[2] ^ mask) * 4 + other) * 16, 16)
                src = buf.at[pl.ds(q, 16), pl.ds(768 + half * 384, 384)]
                copies.append(pltpu.make_async_copy(src, refs[2 + sent].at[slot, other, rows], sems.at[2 + sent]))
    return copies


def gram_x_kernel(place, own, other, mine, theirs, y_basis, *refs):
    high, low, buf, land, core, out_sems, sems, core_sems = refs[6:]

    def load(k):
        src = own if k < 6 else other
        part = pl.ds(k % 6 * 2, 2)
        return pltpu.make_async_copy(src.at[part], land.at[pl.ds(k * 2, 2)], sems.at[k])

    for k in range(12):
        load(k).start()
    for k in range(12):
        load(k).wait()
        for s in (2 * k, 2 * k + 1):
            rows, cols = slice(s // 12 * 1024, s // 12 * 1024 + 1024), slice(s % 12 * 128, s % 12 * 128 + 128)
            high[rows, cols], low[rows, cols] = split(land[s])
    y_high, y_low = split(y_basis[...].T)
    for s in range(12):
        cols = slice(s * 128, s * 128 + 128)
        r_high, r_low = split(mine[:, cols] + theirs[:, cols])
        core[:, cols] = dot3(y_high, y_low, r_high, r_low, ((1,), (1,)))
    for copy in core_copies(place, core, refs, core_sems):
        copy.start()
    for b in range(4):
        rows, cols = slice(b * 256, b * 256 + 256), slice(b * 256, b * 256 + 1280)
        buf[b] = dot3(high[rows, :], low[rows, :], high[cols, :], low[cols, :], ((1,), (1,)))
        send_out(place, buf.at[b], b, lambda x: (x // 2) * 128, refs, out_sems)
    wait_out(refs[:6], out_sems)
    for i in range(4):
        part = refs[i].at[:, :, pl.ds(64, 32)]
        pltpu.make_async_copy(part, part, core_sems.at[i]).wait()


def gram_y_kernel(place, own, other, *refs):
    high, low, buf, out_sems = refs[6:]
    for j in range(16):
        tiles = [
            own[j, half : half + 8, s * 128 : s * 128 + 128] + other[j, 8 - half : 16 - half, s * 128 : s * 128 + 128]
            for half in (0, 8)
            for s in range(12)
        ]
        v = jnp.concatenate(tiles + [jnp.zeros((64, 128), F32)], axis=0).T
        v_high, v_low = split(v)
        for start in (j * 128, 2048 + j * 128):
            if start < 3072:
                high[start : start + 128, :] = v_high
                low[start : start + 128, :] = v_low
    h = place[0]
    for b in range(4):
        starts = [pl.multiple_of((b * 4 + x) * 128 + h * 64, 64) for x in range(4)]
        l_high = jnp.concatenate([high[pl.ds(r, 64), :] for r in starts], axis=0)
        l_low = jnp.concatenate([low[pl.ds(r, 64), :] for r in starts], axis=0)
        cols = slice(b * 512, b * 512 + 1536)
        buf[b] = dot3(l_high, l_low, high[cols, :], low[cols, :], ((1,), (1,)))
        send_out(place, buf.at[b], b, lambda x: x * 128, refs, out_sems)
    wait_out(refs[:6], out_sems)


def gram_pieces(kernel, name, rows, place, args, spaces, scratch, flops):
    ab = jax.ShapeDtypeStruct((2, 4, rows, 384), F32)
    c = jax.ShapeDtypeStruct((2, 16, 16, 384), F32)
    return pl.pallas_call(
        kernel,
        in_specs=[pl.BlockSpec(memory_space=space) for space in (pltpu.SMEM,) + spaces],
        out_specs=[pl.BlockSpec(memory_space=pl.ANY)] * 6,
        out_shape=[ab] * 4 + [c] * 2,
        scratch_shapes=scratch,
        compiler_params=pltpu.CompilerParams(vmem_limit_bytes=VMEM_LIMIT),
        cost_estimate=pl.CostEstimate(flops=flops, bytes_accessed=20000000, transcendentals=0),
        name=name,
    )(place, *args)


GRAM_X_SCRATCH = [
    pltpu.VMEM((2048, 1536), BF16),
    pltpu.VMEM((2048, 1536), BF16),
    pltpu.VMEM((4, 256, 1280), F32),
    pltpu.VMEM((24, 1024, 128), F32),
    pltpu.VMEM((256, 1536), F32),
    pltpu.SemaphoreType.DMA((6,)),
    pltpu.SemaphoreType.DMA((12,)),
    pltpu.SemaphoreType.DMA((4,)),
]
GRAM_Y_SCRATCH = [
    pltpu.VMEM((3072, 256), BF16),
    pltpu.VMEM((3072, 256), BF16),
    pltpu.VMEM((4, 256, 1536), F32),
    pltpu.SemaphoreType.DMA((12,)),
]


def sum4(terms, index):
    return (terms[0][index] + terms[1][index]) + (terms[2][index] + terms[3][index])


def slab_of(v, k):
    return pl.BlockSpec((1,) + v.shape[1:], lambda i: (k, 0, 0, 0))


def shapes_of(px, py):
    return [jax.ShapeDtypeStruct((v.shape[1], v.shape[2] + w.shape[2], 384), F32) for v, w in zip(px, py)]


def add_x_kernel(*refs):
    for kept, came, out in zip(refs[0:3], refs[3:6], refs[6:9]):
        out[...] = kept[0] + came[0]


def add_x(kept, came, shapes):
    return pl.pallas_call(
        add_x_kernel,
        grid=(1,),
        in_specs=[slab_of(v, 1) for v in kept + came],
        out_specs=[pl.BlockSpec(v.shape[1:], lambda i: (0, 0, 0)) for v in kept],
        out_shape=shapes,
        compiler_params=pltpu.CompilerParams(vmem_limit_bytes=VMEM_LIMIT),
        cost_estimate=pl.CostEstimate(flops=400000, bytes_accessed=5000000, transcendentals=0),
        name="add_x",
    )(*kept, *came)


def add_y_kernel(*refs):
    for kept, came, out in zip(refs[0:3], refs[3:6], refs[9:12]):
        out[...] = kept[0] + came[0]


def add_y(kept, came, sums):
    ins, outs = [], []
    for v, total in zip(kept, sums):
        rows = v.shape[2] // 2
        first = total.shape[1] // rows - 2
        ins.append(pl.BlockSpec((1, v.shape[1], rows, 384), lambda i: (1, 0, i, 0)))
        outs.append(pl.BlockSpec((v.shape[1], rows, 384), lambda i, first=first: (0, first + i, 0)))
    return pl.pallas_call(
        add_y_kernel,
        grid=(2,),
        in_specs=ins + ins + [pl.BlockSpec(memory_space=pl.ANY)] * 3,
        out_specs=outs,
        out_shape=[jax.ShapeDtypeStruct(v.shape, F32) for v in sums],
        input_output_aliases={6: 0, 7: 1, 8: 2},
        compiler_params=pltpu.CompilerParams(vmem_limit_bytes=VMEM_LIMIT),
        cost_estimate=pl.CostEstimate(flops=300000, bytes_accessed=4000000, transcendentals=0),
        name="add_y",
    )(*kept, *came, *sums)


def add_own_kernel(*refs):
    for k_x, c_x, k_y, c_y, out in zip(refs[0:3], refs[3:6], refs[6:9], refs[9:12], refs[12:15]):
        rows = k_x.shape[2]
        out[:, :rows, :] = k_x[0] + c_x[0]
        out[:, rows:, :] = k_y[0] + c_y[0]


def add_own(terms, shapes):
    return pl.pallas_call(
        add_own_kernel,
        grid=(1,),
        in_specs=[slab_of(v, 0) for v in terms],
        out_specs=[pl.BlockSpec(v.shape, lambda i: (0, 0, 0)) for v in shapes],
        out_shape=shapes,
        compiler_params=pltpu.CompilerParams(vmem_limit_bytes=VMEM_LIMIT),
        cost_estimate=pl.CostEstimate(flops=700000, bytes_accessed=9000000, transcendentals=0),
        name="add_own",
    )(*terms)


def sum_first_kernel(place, own_a, last_a, own_b, last_b, *outs):
    for axis, own, last, out in ((2, own_a, last_a, outs[0:2]), (1, own_b, last_b, outs[2:4])):
        for sent, slot, mask in owner_masks(place):
            k = place[axis] ^ mask
            out[sent][slot] = own[k] + last[k]


def add_two_kernel(place, first, second, out):
    out[...] = first[...] + second[...]


def add_second_kernel(place, k_a, c_a, k_b, c_b, out_a, out_b):
    out_a[...] = k_a[1] + c_a[1]
    out_b[...] = k_b[1] + c_b[1]


def sum_second_kernel(place, *refs):
    outs = refs[6:]
    for part in range(2):
        kept, came, last = refs[part * 3 : part * 3 + 3]

        def total(rows):
            return (kept[0, rows, :] + came[0, rows, :]) + last[rows, :]

        for d in range(4):
            for g in range(2):
                to = part * 32 + g * 16
                rows = pl.ds(pl.multiple_of(g * 96 + ahead(place, 3, d) * 16, 16), 16)
                outs[d][to : to + 16, :] = total(rows)
        outs[4][part * 32 : part * 32 + 32, :] = total(slice(64, 96))


def sum_last_kernel(place, *refs):
    slots, direct_x, keep, give, wide = refs[5:]
    h = place[0]
    j = place[2] * 4 + place[1]
    block_x = h * 8 + j // 2
    parts = [sum4(refs[:4], (slice(0, 32), slice(None))), sum4(refs[:4], (slice(32, 64), slice(None))), refs[4][...]]
    zero = jnp.zeros((16, 128), F32)
    for k in range(16):
        lane = k % 3 * 128
        tile_x = parts[k // 3][:16, lane : lane + 128] if k < 9 else zero
        tile_y = parts[k // 3][16:, lane : lane + 128] if k < 9 else zero
        to_x, to_y = lax.rem(block_x + k, 16), lax.rem(j + k, 16)
        direct_x[to_x] = tile_x
        wide[lax.rem(to_y + 8 * h, 16)] = tile_y
        for e in range(2):
            half = tile_x[:, e * 64 : e * 64 + 64]
            slots[2 * to_x + e, 16:] = jnp.concatenate([half[:8], half[8:]], axis=1)
            slots[16 * e + to_y, :16] = tile_y
    keep[...] = wide[:8]
    give[...] = wide[8:]


def select_kernel(place, got, direct_x, keep, come, out):
    h = place[0]
    j = place[2] * 4 + place[1]
    block_x = h * 8 + j // 2
    for block in range(16):
        first, second = got[2 * block, 16:], got[2 * block + 1, 16:]
        turned = jnp.concatenate(
            [jnp.concatenate([t[:, :64] for t in (first, second)], axis=1), jnp.concatenate([t[:, 64:] for t in (first, second)], axis=1)],
            axis=0,
        )
        out[block] = jnp.where(lax.rem(block - block_x + 16, 16) <= 8, direct_x[block], turned)
    for block in range(8):
        is_direct = lax.rem(h * 8 + block - j + 16, 16) <= 8
        for half in range(2):
            direct = jnp.where(h == half, keep[block], come[block])
            out[16 + 2 * block + half] = jnp.where(is_direct, direct, got[half * 16 + h * 8 + block, :16])


def assemble_kernel(scale_x, scale_y, place, q0, q1, q2, q3, gram_x, gram_y, rows):
    h = place[0]
    j = place[2] * 4 + place[1]
    block_x = h * 8 + j // 2
    for quarter, mask in zip((q0, q1, q2, q3), (0, place[4], 4 - place[4], 2)):
        z = place[3] ^ mask
        rows[:, pl.ds(pl.multiple_of(z * 16, 16), 16), :] = quarter[...]
    for block in range(16):
        direct = rows[block]
        turned = direct.T
        turned = jnp.concatenate([turned[:64], turned[64:]], axis=1)
        is_direct = lax.rem(block - block_x + 16, 16) <= 8
        gram_x[:, block * 128 : block * 128 + 128] = jnp.where(is_direct, direct, turned) * scale_x
    for block in range(8):
        direct = jnp.concatenate([rows[16 + 2 * block], rows[17 + 2 * block]], axis=0)
        is_direct = lax.rem(h * 8 + block - j + 16, 16) <= 8
        gram_y[:, block * 128 : block * 128 + 128] = jnp.where(is_direct, direct, direct.T) * scale_y


def small_kernel(kernel, name, out_shape, scratch, *args):
    return pl.pallas_call(
        kernel,
        in_specs=[pl.BlockSpec(memory_space=pltpu.SMEM)] + [pl.BlockSpec(memory_space=pltpu.VMEM)] * (len(args) - 1),
        out_shape=out_shape,
        scratch_shapes=scratch,
        compiler_params=pltpu.CompilerParams(vmem_limit_bytes=VMEM_LIMIT),
        name=name,
    )(*args)


def per_device(species_field, x_mode_basis, y_mode_basis):
    h, j, z0 = lax.axis_index("gx"), lax.axis_index("gy"), lax.axis_index("gz")
    x0, y0 = j % 4, j // 4
    place = jnp.stack([h, x0, y0, z0, 1 + 2 * h]).astype(jnp.int32)
    nx = 2 * species_field.shape[1]
    ny = 16 * species_field.shape[2]
    slices = 4 * species_field.shape[0]
    ranks = x_mode_basis.shape[1]

    other_field = lax.ppermute(species_field, "gx", SWAP)
    mine, give, both = project(place, species_field, x_mode_basis)
    theirs = lax.ppermute(give, "gx", SWAP)
    fibers = lax.all_to_all(both, "gy", 0, 0, tiled=True)

    def first_swaps(pieces):
        return [swap(pieces[2 * i + 1], 0) for i, swap in enumerate((swap_x, swap_y, swap_z))]

    px = gram_pieces(
        gram_x_kernel, "gram_x", 96, place, (species_field, other_field, mine, theirs, y_mode_basis),
        (pl.ANY, pl.ANY, pltpu.VMEM, pltpu.VMEM, pltpu.VMEM), GRAM_X_SCRATCH, 12000000000,
    )
    came_x = first_swaps(px)
    _, fibers = lax.optimization_barrier((px, fibers))
    other_fibers = lax.ppermute(fibers, "gx", SWAP)
    py = gram_pieces(
        gram_y_kernel, "gram_y", 64, place, (fibers, other_fibers), (pltpu.VMEM, pltpu.VMEM), GRAM_Y_SCRATCH, 2400000000
    )
    came_y = first_swaps(py)

    kept_x, kept_y = list(px[0::2]), list(py[0::2])
    shapes = shapes_of(kept_x, kept_y)
    last = add_y(kept_y, came_y, add_x(kept_x, came_x, shapes))
    *terms, last = lax.optimization_barrier((*kept_x, *came_x, *kept_y, *came_y, last))
    own_a, own_b, own_c = add_own(terms, shapes)
    last_a, last_b, last_c = [swap(v, 1) for v, swap in zip(last, (swap_x, swap_y, swap_z))]
    halves = jax.ShapeDtypeStruct((2, 160, 384), F32)
    kept_a, sent_a, kept_b, sent_b = small_kernel(
        sum_first_kernel, "sum_first", [halves] * 4, [], place, own_a, last_a, own_b, last_b
    )
    came_a, came_b = swap_y(sent_a, 0), swap_x(sent_b, 0)
    last_c, kept_a = lax.optimization_barrier((last_c, kept_a))
    c = small_kernel(add_two_kernel, "sum_last_third", shapes[2], [], place, own_c, last_c)
    c = lax.all_to_all(c, "gy", 0, 0, tiled=True).sum(axis=0)
    second = jax.ShapeDtypeStruct((160, 384), F32)
    last_a, last_b = small_kernel(
        add_second_kernel, "add_second", [second] * 2, [], place, kept_a, came_a, kept_b, came_b
    )
    part = jax.ShapeDtypeStruct((64, 384), F32)
    *quarters, core = small_kernel(
        sum_second_kernel, "sum_second", [part] * 5, [],
        place, kept_a, came_a, swap_y(last_a, 1), kept_b, came_b, swap_x(last_b, 1),
    )
    blocks = jax.ShapeDtypeStruct((8, 16, 128), F32)
    slots, direct_x, keep, give = small_kernel(
        sum_last_kernel, "sum_last",
        [jax.ShapeDtypeStruct((32, 24, 128), F32), jax.ShapeDtypeStruct((16, 16, 128), F32), blocks, blocks],
        [pltpu.VMEM((16, 16, 128), F32)],
        place, *[quarters[0]] + [shift_z(quarters[d], d) for d in (1, 2, 3)], c,
    )
    core = core.reshape(2, 2, 16, 3, 128).transpose(4, 0, 1, 3, 2).reshape(128, 12, 16)

    got = lax.all_to_all(slots, ("gx", "gy"), 0, 0, tiled=True)
    come = lax.ppermute(give, "gx", SWAP)
    part = small_kernel(
        select_kernel, "select", jax.ShapeDtypeStruct((32, 16, 128), F32), [], place, got, direct_x, keep, come
    )
    first = swap_z(part, 0)
    quarters = [part, first, swap_z(part, 1), shift_z(part, 2)]
    gram_x, gram_y = small_kernel(
        functools.partial(assemble_kernel, 1.0 / (ny * slices), 1.0 / (ranks * slices)),
        "assemble",
        [jax.ShapeDtypeStruct((64, nx), F32), jax.ShapeDtypeStruct((128, ny // 2), F32)],
        [pltpu.VMEM((32, 64, 128), F32)],
        place, *quarters,
    )
    return (gram_x, gram_y, core)


def solution(mesh):
    in_specs = (P("gz", "gx", "gy"), P("gx", None), P("gy", None))
    out_specs = (P(("gx", "gy"), None), P("gy", "gx"), P("gx", "gz", "gy"))
    return jax.shard_map(
        per_device, mesh=mesh, in_specs=in_specs, out_specs=out_specs, check_vma=False
    )
```
